32 devices in a mesh: dp: 4 (over y, x), tm: 8 (over z, core).
Axes of the slice: x: 2, y: 2, z: 4, core: 2. Of those that a mesh axis runs over, the one named last changes fastest.
Arguments:
- records: bfloat16 [4, 1024, 1024], P('dp', 'tm'), may hold values from -6 to 6
- x_weight: bfloat16 [1024, 512], replicated, may hold values from -0.1875 to 0.1875
- bc_weight: bfloat16 [1024, 256], replicated, may hold values from -0.1875 to 0.1875
- decay_codes: int32 [4, 1024, 8], P('dp', 'tm'), may hold values from 0 to 524
- out_grad: bfloat16 [4, 1024, 512], P('dp', 'tm'), may hold values from -6 to 6
Outputs:
- y_out: bfloat16 [4, 1024, 512], P('dp', 'tm')
- x_grad: float32 [1024, 512], P('tm')
- bc_grad: float32 [1024, 256], P('tm')
The draws below stay inside these ranges and needn't reach their ends.
All inputs are finite; a program needn't handle non-finite values.
Results may differ from the reference program's by a relative error of at most 0.0085.
Values sent between devices are 32-bit elements; how exact they have to be, the bound alone decides.
A program may use at most 64 MiB of HBM per device.

```python
import jax
import jax.numpy as jnp
from jax import lax

D = 1024
HEADS = 8
HEAD = 64
STATE = 128
SPAN = 128
LD = 128
FRAMES = 1024
RECS = 4


def draw_decay_codes(key, part):
    level_key = jax.random.fold_in(key, 11)
    rough_key = jax.random.fold_in(key, 23)
    blocks = FRAMES // LD
    powers = jax.random.randint(level_key, (RECS, blocks, 1, HEADS), 0, 11)
    levels = jnp.minimum(jnp.left_shift(jnp.ones_like(powers), powers) - 1, 524)
    rough = jax.random.randint(rough_key, (RECS, blocks, LD, HEADS), 0, 13)
    codes = jnp.minimum(levels + rough, 524)
    return codes.reshape(RECS, FRAMES, HEADS).astype(jnp.int32)


def block_scale(stream_key, shape, cuts, smallest, largest):
    def one(dim, parts):
        draws = jax.random.uniform(jax.random.fold_in(jax.random.fold_in(stream_key, 6), dim), (parts,), jnp.float32, smallest / len(cuts), largest / len(cuts))
        return jnp.repeat(jnp.exp(draws), shape[dim] // parts).reshape((-1,) + (1,) * (len(shape) - dim - 1))

    level = one(*cuts[0])
    for cut in cuts[1:]:
        level = level * one(*cut)
    return level


def centred(own_key, shape, deviation, most, shards=(), held_as=jnp.bfloat16):
    drawn = deviation * jax.random.normal(own_key, shape, jnp.float32)
    if shards:
        drawn = drawn * block_scale(own_key, shape, shards, -0.22, 0.18)
    return jnp.clip(drawn, -most, most).astype(held_as)


def setup_inputs(seed: int = 0) -> dict:
    keys = jax.random.split(jax.random.key(seed), 6)
    return {
        "records": centred(keys[0], (RECS, FRAMES, D), 1.0, 6.0, ((0, 4), (1, 8))),
        "x_weight": centred(keys[1], (D, HEADS * HEAD), D ** -0.5, 0.1875),
        "bc_weight": centred(keys[2], (D, 2 * STATE), D ** -0.5, 0.1875),
        "decay_codes": draw_decay_codes(jax.random.fold_in(keys[5], 71), 0),
        "out_grad": centred(keys[4], (RECS, FRAMES, HEADS * HEAD), 1.0, 6.0, ((0, 4), (1, 8))),
    }


highest = lax.Precision.HIGHEST


def span_kernel(log_decay):
    running = jnp.cumsum(log_decay, axis=1)
    length = log_decay.shape[1]
    causal = lax.broadcasted_iota(jnp.int32, (length, length), 0) >= lax.broadcasted_iota(jnp.int32, (length, length), 1)
    causal = causal[None, None, :, :]
    heads_first = jnp.transpose(running, (0, 2, 1))
    gaps = heads_first[:, :, :, None] - heads_first[:, :, None, :]
    kernel = jnp.where(causal, jnp.exp(jnp.where(causal, gaps, 0.0)), 0.0)
    return running, kernel


def block_scores(readout, inject):
    return jnp.einsum("rtn,rsn->rts", readout.astype(jnp.bfloat16), inject.astype(jnp.bfloat16), preferred_element_type=jnp.float32)


def forward_span(carry_state, pieces):
    mixer_f, inject, readout, cot_heads, log_decay = pieces
    running, kernel = span_kernel(log_decay)
    scores = block_scores(readout, inject)
    mixing = kernel * scores[:, None, :, :]
    decayed = jnp.exp(running)
    within = jnp.einsum("rhts,rshp->rthp", mixing, mixer_f, precision=highest)
    carried = decayed[..., None] * jnp.einsum("rhpn,rtn->rthp", carry_state, readout, precision=highest)
    pair_dots = jnp.einsum("rthp,rshp->rhts", cot_heads, mixer_f, precision=highest)
    grad_read = jnp.einsum("rhts,rsn->rtn", kernel * pair_dots, inject, precision=highest)
    grad_read = grad_read + jnp.einsum("rthp,rhpn->rtn", decayed[..., None] * cot_heads, carry_state, precision=highest)
    to_end = jnp.exp(running[:, -1:, :] - running)
    new_state = jnp.exp(running[:, -1, :])[:, :, None, None] * carry_state
    new_state = new_state + jnp.einsum("rshp,rsn->rhpn", to_end[..., None] * mixer_f, inject, precision=highest)
    return new_state, (within + carried, grad_read)


def reverse_span(adjoint, pieces):
    mixer_f, inject, readout, cot_heads, log_decay = pieces
    running, kernel = span_kernel(log_decay)
    scores = block_scores(readout, inject)
    mixing = kernel * scores[:, None, :, :]
    pair_dots = jnp.einsum("rthp,rshp->rhts", cot_heads, mixer_f, precision=highest)
    to_end = jnp.exp(running[:, -1:, :] - running)
    grad_mixer = jnp.einsum("rhts,rthp->rshp", mixing, cot_heads, precision=highest)
    grad_mixer = grad_mixer + to_end[..., None] * jnp.einsum("rhpn,rsn->rshp", adjoint, inject, precision=highest)
    grad_inject = jnp.einsum("rhts,rtn->rsn", kernel * pair_dots, readout, precision=highest)
    grad_inject = grad_inject + jnp.einsum("rshp,rhpn->rsn", to_end[..., None] * mixer_f, adjoint, precision=highest)
    new_adjoint = jnp.exp(running[:, -1, :])[:, :, None, None] * adjoint
    new_adjoint = new_adjoint + jnp.einsum("rthp,rtn->rhpn", jnp.exp(running)[..., None] * cot_heads, readout, precision=highest)
    return new_adjoint, (grad_mixer, grad_inject)


def to_blocks(array, frames):
    return array.reshape((frames // SPAN, 1, SPAN) + array.shape[1:])


def reference(records, x_weight, bc_weight, decay_codes, out_grad):
    out_scale = (STATE * FRAMES) ** -0.5
    grad_scale = (RECS * FRAMES) ** -0.5
    decay_unit = 1.0 / (32.0 * FRAMES)

    def record_pass(pieces):
        signal, codes, cot_in = pieces
        mixer_in = jnp.dot(signal, x_weight, preferred_element_type=jnp.float32).astype(jnp.bfloat16)
        state_proj = jnp.dot(signal, bc_weight, preferred_element_type=jnp.float32).astype(jnp.bfloat16)
        log_decay = -decay_unit * codes.astype(jnp.float32)
        cotangent = cot_in.astype(jnp.float32) * out_scale
        mixer_f = mixer_in.astype(jnp.float32).reshape(FRAMES, HEADS, HEAD)
        inject = state_proj[:, :STATE].astype(jnp.float32)
        readout = state_proj[:, STATE:].astype(jnp.float32)
        cot_heads = cotangent.reshape(FRAMES, HEADS, HEAD)
        blocks = (to_blocks(mixer_f, FRAMES), to_blocks(inject, FRAMES), to_blocks(readout, FRAMES),
                  to_blocks(cot_heads, FRAMES), to_blocks(log_decay, FRAMES))
        zero_state = jnp.zeros((1, HEADS, HEAD, STATE), jnp.float32)
        ignored, (local_out, local_read) = lax.scan(forward_span, zero_state, blocks)
        ignored_too, (local_grad, local_inject) = lax.scan(reverse_span, zero_state, blocks, reverse=True)
        output = local_out.reshape(FRAMES, HEADS * HEAD).astype(jnp.bfloat16)
        grad_mix = local_grad.reshape(FRAMES, HEADS * HEAD).astype(jnp.bfloat16)
        grad_proj = jnp.concatenate([local_inject.reshape(FRAMES, STATE), local_read.reshape(FRAMES, STATE)], axis=1).astype(jnp.bfloat16)
        grad_cat = jnp.concatenate([grad_mix, grad_proj], axis=1)
        term = jnp.dot(signal.T, grad_cat, preferred_element_type=jnp.float32)
        return output, term

    outputs, terms = lax.map(record_pass, (records, decay_codes, out_grad))
    summed = jnp.sum(terms, axis=0) * grad_scale
    return outputs, summed[:, :HEADS * HEAD], summed[:, HEADS * HEAD:]
```

```python
import functools

import jax
import jax.numpy as jnp
from jax import lax
from jax.experimental import pallas as pl
from jax.experimental.pallas import tpu as pltpu
from jax.sharding import PartitionSpec as P

MESH = pl.DeviceIdType.MESH
CHUNKS = 4
f32 = jnp.float32
bf16 = jnp.bfloat16


def dot(a, b, left=1, right=0):
    return lax.dot_general(
        a, b, (((left,), (right,)), ((), ())), preferred_element_type=f32
    )


def kernel(
    groups, tm, rec_ref, xw_ref, bw_ref, code_ref, og_ref, y_ref, out_ref,
    rec_all, carry, adj, ends, starts, sent_f, sent_b, keep,
    gt, gall, pt, pbuf, qs, rbuf, fin, ylocal, glocal,
    rec_s, rec_r, f_s, f_r, b_s, b_r, g_s, g_r, c_s, c_r, z_s, z_r, o_s, o_r,
):
    frames, heads = code_ref.shape
    width = xw_ref.shape[1]
    head = width // heads
    state = bw_ref.shape[1] // 2
    rows = out_ref.shape[2]
    block = out_ref.shape[1]
    chips = tm // 2
    unit = 1.0 / (32.0 * frames * tm)
    scale = (state * frames * tm) ** (-0.5)

    d = lax.axis_index("dp")
    i = lax.axis_index("tm")
    z = i // 2
    core = i % 2
    partner = i + 1 - 2 * core
    other = i - 1 + 2 * core
    has_other = jnp.logical_and(other >= 0, other < tm)

    barrier = pltpu.get_barrier_semaphore()

    def greet(dp_to, tm_to):
        pl.semaphore_signal(barrier, inc=1, device_id=(dp_to, tm_to), device_id_type=MESH)

    for k in range(1, groups):
        greet(lax.rem(d + k, groups), i)
    for k in range(1, chips):
        greet(d, lax.rem(z + k, chips) * 2 + core)
    greet(d, partner)

    @pl.when(has_other)
    def _():
        greet(d, other)

    rec = rec_ref[...]
    rec_all[d] = rec.astype(f32)
    fixed = (groups - 1) + (chips - 1) + 1
    pl.semaphore_wait(barrier, fixed + has_other.astype(jnp.int32))

    def remote(src, dst, send, recv, dp_to, tm_to):
        return pltpu.make_async_remote_copy(
            src_ref=src, dst_ref=dst, send_sem=send, recv_sem=recv,
            device_id=(dp_to, tm_to), device_id_type=MESH,
        )

    rec_copies = []
    for k in range(1, groups):
        copy = remote(rec_all.at[d], rec_all.at[d], rec_s.at[k], rec_r.at[k],
                      lax.rem(d + k, groups), i)
        copy.start()
        rec_copies.append(copy)

    mix = dot(rec, xw_ref[...]).astype(bf16)
    proj = dot(rec, bw_ref[...]).astype(bf16)
    inject, readout = proj[:, :state], proj[:, state:]
    og = og_ref[...]
    mix_t = mix.astype(f32).T
    cot_t = og.astype(f32).T
    proj_t = proj.astype(f32).T.astype(bf16)

    codes = code_ref[...].astype(f32)
    high = jnp.floor(codes * 0.125)
    low = codes - 8.0 * high
    spread = (
        lax.broadcasted_iota(jnp.int32, (heads, width), 1) // head
        == lax.broadcasted_iota(jnp.int32, (heads, width), 0)
    ).astype(f32)
    high_w, low_w = dot(high, spread), dot(low, spread)
    t_at = lax.broadcasted_iota(jnp.int32, (frames, frames), 0)
    s_at = lax.broadcasted_iota(jnp.int32, (frames, frames), 1)
    causal = t_at >= s_at
    tri = causal.astype(f32).astype(bf16)
    upper_tri = (t_at <= s_at).astype(f32).astype(bf16)
    sums = jnp.concatenate([upper_tri, jnp.ones((frames, frames), bf16)], axis=1)
    run = 8.0 * dot(tri, high_w.astype(bf16)) + dot(tri, low_w.astype(bf16))
    both = 8.0 * dot(high_w.T.astype(bf16), sums) + dot(low_w.T.astype(bf16), sums)
    run_t, total_t = both[:, :frames], both[:, frames:]
    decayed_t = jnp.exp(-unit * run_t)
    to_end_t = jnp.exp(-unit * (total_t - run_t))
    keep[...] = jnp.exp(-unit * total_t)
    mix_end = (to_end_t * mix_t).astype(bf16)
    cot_dec = (decayed_t * cot_t).astype(bf16)
    ends[...] = dot(mix_end, inject)
    starts[...] = dot(cot_dec, readout)

    part = width // CHUNKS

    def chain(first, last, target, arrive, own, sent, send_sem, recv_sem):
        for c in range(CHUNKS):
            at = pl.ds(c * part, part)
            copy = remote(sent.at[at], arrive.at[at], send_sem.at[c], recv_sem.at[c], d, target)

            @pl.when(jnp.logical_not(first))
            def _():
                copy.wait_recv()

            @pl.when(first)
            def _():
                arrive[at] = jnp.zeros((part, state), f32)

            @pl.when(jnp.logical_not(last))
            def _():
                sent[at] = keep[at] * arrive[at] + own[at]
                copy.start()

    def forward():
        chain(i == 0, i == tm - 1, lax.rem(i + 1, tm), carry, ends, sent_f, f_s, f_r)

    def backward():
        chain(i == tm - 1, i == 0, lax.rem(i + tm - 1, tm), adj, starts, sent_b, b_s, b_r)

    lower = i < tm // 2
    middle = jnp.logical_or(i == tm // 2 - 1, i == tm // 2)
    low_early = jnp.logical_and(lower, jnp.logical_not(middle))
    high_early = jnp.logical_and(jnp.logical_not(lower), jnp.logical_not(middle))
    pl.when(low_early)(forward)
    pl.when(high_early)(backward)

    scores = dot(readout, inject, 1, 1)
    cot_tb = cot_t.astype(bf16)
    pairs = jnp.zeros((frames, frames), f32)
    for h in range(heads):
        cols = slice(h * head, (h + 1) * head)
        gap = run[:, h * head:h * head + 1] - run_t[h * head:h * head + 1, :]
        decay = jnp.where(causal, jnp.exp(-unit * gap), 0.0)
        mixing = (decay * scores).astype(bf16)
        ylocal[:, cols] = dot(mixing, mix[:, cols])
        pairs = pairs + decay * dot(og[:, cols], mix[:, cols], 1, 1)
        glocal[cols, :] = dot(cot_tb[cols, :], mixing)
    pairs = pairs.astype(bf16)
    inj_local = dot(proj_t[state:], pairs)
    read_local = dot(proj_t[:state], pairs, 1, 1)

    pl.when(jnp.logical_and(lower, middle))(forward)
    pl.when(jnp.logical_not(high_early))(backward)
    pl.when(jnp.logical_not(lower))(forward)

    adj_b = adj[...].astype(bf16)
    carry_b = carry[...].astype(bf16)
    mixer_grad = to_end_t * dot(adj_b, inject, 1, 1) + glocal[...]
    inj_grad = inj_local + dot(adj_b, mix_end, 0, 0)
    read_grad = read_local + dot(carry_b, cot_dec, 0, 0)

    def rounded(a):
        return (scale * a).astype(bf16).astype(f32)

    gt[0:width] = rounded(mixer_grad)
    gt[width:width + state] = rounded(inj_grad)
    gt[width + state:width + 2 * state] = rounded(read_grad)

    g_copies = []
    for k in range(1, groups):
        to = lax.rem(d + k, groups)
        copy = remote(gt.at[pl.ds(pl.multiple_of(to * block, 8), block)], gall.at[d],
                      g_s.at[k], g_r.at[k], to, i)
        copy.start()
        g_copies.append(copy)
    gall[d] = gt[pl.ds(pl.multiple_of(d * block, 8), block)]
    y_ref[...] = (
        jnp.exp(-unit * run) * dot(readout, carry_b, 1, 1) + ylocal[...]
    ).astype(bf16)
    for copy in rec_copies:
        copy.wait_recv()
    for copy in g_copies:
        copy.wait_recv()

    lhs = jnp.concatenate([gall[r].astype(bf16) for r in range(groups)], axis=1)
    c_copies = []
    for zt in range(chips):
        rhs = jnp.concatenate(
            [rec_all[r][:, zt * 2 * rows:(zt + 1) * 2 * rows].astype(bf16) for r in range(groups)],
            axis=0,
        )
        prod = dot(lhs, rhs)
        pt[0, zt] = prod[:, :rows]
        pt[1, zt] = prod[:, rows:]
        copy = remote(pt.at[1 - core, zt], pbuf.at[zt], c_s.at[zt], c_r.at[zt], d, partner)
        copy.start()
        c_copies.append(copy)
    for copy in c_copies:
        copy.wait_recv()
    z_copies = []
    for k in range(1, chips):
        zt = lax.rem(z + k, chips)
        qs[k] = pt[core, zt] + pbuf[zt]
        copy = remote(qs.at[k], rbuf.at[k], z_s.at[k], z_r.at[k], d, zt * 2 + core)
        copy.start()
        z_copies.append(copy)
    total = pt[core, z] + pbuf[z]
    for k, copy in enumerate(z_copies, 1):
        copy.wait_recv()
        total = total + rbuf[k]
    fin[d] = total
    o_copies = []
    for k in range(1, groups):
        copy = remote(fin.at[d], fin.at[d], o_s.at[k], o_r.at[k], lax.rem(d + k, groups), i)
        copy.start()
        o_copies.append(copy)
    for copy in o_copies:
        copy.wait_recv()
    out_ref[...] = fin[...]

    for copy in rec_copies + g_copies + c_copies + z_copies + o_copies:
        copy.wait_send()

    for c in range(CHUNKS):
        at = pl.ds(c * part, part)

        @pl.when(i < tm - 1)
        def _():
            remote(sent_f.at[at], carry.at[at], f_s.at[c], f_r.at[c], d, lax.rem(i + 1, tm)).wait_send()

        @pl.when(i > 0)
        def _():
            remote(sent_b.at[at], adj.at[at], b_s.at[c], b_r.at[c], d, lax.rem(i + tm - 1, tm)).wait_send()


def body(records, x_weight, bc_weight, decay_codes, out_grad):
    signal = records[0]
    codes = decay_codes[0]
    frames, model = signal.shape
    width = x_weight.shape[1]
    wide = width + bc_weight.shape[1]
    state = bc_weight.shape[1] // 2
    tm = lax.axis_size("tm")
    groups = lax.axis_size("dp")
    chips = tm // 2
    rows = model // tm
    block = wide // groups
    grad_scale = (groups * frames * tm) ** (-0.5)
    vmem = pl.BlockSpec(memory_space=pltpu.VMEM)

    def buf(*shape):
        return pltpu.VMEM(shape, f32)

    def sems(n):
        return [pltpu.SemaphoreType.DMA((n,)), pltpu.SemaphoreType.DMA((n,))]

    y, out = pl.pallas_call(
        functools.partial(kernel, groups, tm),
        out_shape=(
            jax.ShapeDtypeStruct((frames, width), bf16),
            jax.ShapeDtypeStruct((groups, block, rows), f32),
        ),
        in_specs=[vmem] * 5,
        out_specs=(vmem, vmem),
        scratch_shapes=[
            buf(groups, frames, model),
            buf(width, state), buf(width, state), buf(width, state), buf(width, state),
            buf(width, state), buf(width, state), buf(width, state),
            buf(wide, frames), buf(groups, block, frames),
            buf(2, chips, block, rows), buf(chips, block, rows),
            buf(chips, block, rows), buf(chips, block, rows),
            buf(groups, block, rows), buf(frames, width), buf(width, frames),
            *sems(groups), *sems(CHUNKS), *sems(CHUNKS), *sems(groups),
            *sems(chips), *sems(chips), *sems(groups),
        ],
        compiler_params=pltpu.CompilerParams(
            collective_id=0, has_side_effects=True, vmem_limit_bytes=50 * 1024 * 1024
        ),
    )(signal, x_weight, bc_weight, codes, out_grad[0])
    out = out.reshape(wide, rows).T * grad_scale
    return (y[None], out[:, :width], out[:, width:])


def solution(mesh):
    return jax.shard_map(
        body,
        mesh=mesh,
        in_specs=(P("dp", "tm", None), P(), P(), P("dp", "tm", None), P("dp", "tm", None)),
        out_specs=(P("dp", "tm", None), P("tm", None), P("tm", None)),
        check_vma=False,
    )
```

```python
import functools

import jax
import jax.numpy as jnp
from jax import lax
from jax.experimental import pallas as pl
from jax.experimental.pallas import tpu as pltpu
from jax.sharding import PartitionSpec as P

MESH = pl.DeviceIdType.MESH
CHUNKS = 4
PIECES = 3
f32 = jnp.float32
bf16 = jnp.bfloat16


def dot(a, b, left=1, right=0):
    return lax.dot_general(
        a, b, (((left,), (right,)), ((), ())), preferred_element_type=f32
    )


def kernel(
    groups, tm, rec_hbm, xw_hbm, bw_hbm, code_hbm, og_hbm, y_ref, out_ref,
    rec_ref, xw_ref, bw_ref, code_ref, og_ref, in_s, rec_all, rhs, carry, adj, ends, starts, sent_f, sent_b, keep,
    gt, gall, pt, pbuf, qs, rbuf, fin, ylocal, glocal,
    rec_s, rec_r, f_s, f_r, b_s, b_r, g_s, g_r, c_s, c_r, z_s, z_r, o_s, o_r,
):
    heads, frames = code_ref.shape
    width = xw_ref.shape[1]
    head = width // heads
    state = bw_ref.shape[1] // 2
    piece, rows = out_ref.shape[2:]
    block = PIECES * piece
    chips = tm // 2
    unit = 1.0 / (32.0 * frames * tm)
    scale = (state * frames * tm) ** (-0.5)

    loads = []
    for n, (src, dst) in enumerate((
        (rec_hbm, rec_ref), (bw_hbm, bw_ref), (xw_hbm, xw_ref), (code_hbm, code_ref), (og_hbm, og_ref),
    )):
        load = pltpu.make_async_copy(src, dst, in_s.at[n])
        load.start()
        loads.append(load)

    d = lax.axis_index("dp")
    i = lax.axis_index("tm")
    z = i // 2
    core = i % 2
    partner = i + 1 - 2 * core
    other = i - 1 + 2 * core
    has_other = jnp.logical_and(other >= 0, other < tm)

    barrier = pltpu.get_barrier_semaphore()

    def greet(dp_to, tm_to):
        pl.semaphore_signal(barrier, inc=1, device_id=(dp_to, tm_to), device_id_type=MESH)

    for k in range(1, groups):
        greet(lax.rem(d + k, groups), i)
    for k in range(1, chips):
        greet(d, lax.rem(z + k, chips) * 2 + core)
    greet(d, partner)

    @pl.when(has_other)
    def _():
        greet(d, other)

    loads[0].wait()
    rec = rec_ref[...]
    rec_all[d] = rec.astype(f32)
    fixed = (groups - 1) + (chips - 1) + 1
    pl.semaphore_wait(barrier, fixed + has_other.astype(jnp.int32))

    def remote(src, dst, send, recv, dp_to, tm_to):
        return pltpu.make_async_remote_copy(
            src_ref=src, dst_ref=dst, send_sem=send, recv_sem=recv,
            device_id=(dp_to, tm_to), device_id_type=MESH,
        )

    rec_copies = []
    for k in range(1, groups):
        copy = remote(rec_all.at[d], rec_all.at[d], rec_s.at[k], rec_r.at[k],
                      lax.rem(d + k, groups), i)
        copy.start()
        rec_copies.append(copy)

    for load in loads[1:]:
        load.wait()
    mix = dot(rec, xw_ref[...]).astype(bf16)
    proj = dot(rec, bw_ref[...]).astype(bf16)
    inject, readout = proj[:, :state], proj[:, state:]
    og = og_ref[...]
    mix_t = mix.astype(f32).T
    cot_t = og.astype(f32).T
    proj_t = proj.astype(f32).T.astype(bf16)

    codes = code_ref[...].astype(f32)
    high = jnp.floor(codes * 0.125)
    low = codes - 8.0 * high
    spread = (
        lax.broadcasted_iota(jnp.int32, (heads, width), 1) // head
        == lax.broadcasted_iota(jnp.int32, (heads, width), 0)
    ).astype(f32)
    high_w, low_w = dot(high, spread, 0, 0), dot(low, spread, 0, 0)
    high_t, low_t = dot(spread, high, 0, 0), dot(spread, low, 0, 0)
    t_at = lax.broadcasted_iota(jnp.int32, (frames, frames), 0)
    s_at = lax.broadcasted_iota(jnp.int32, (frames, frames), 1)
    causal = t_at >= s_at
    tri = causal.astype(f32).astype(bf16)
    upper_tri = (t_at <= s_at).astype(f32).astype(bf16)
    sums = jnp.concatenate([upper_tri, jnp.ones((frames, frames), bf16)], axis=1)
    run = 8.0 * dot(tri, high_w.astype(bf16)) + dot(tri, low_w.astype(bf16))
    both = 8.0 * dot(high_t.astype(bf16), sums) + dot(low_t.astype(bf16), sums)
    run_t, total_t = both[:, :frames], both[:, frames:]
    decayed_t = jnp.exp(-unit * run_t)
    to_end_t = jnp.exp(-unit * (total_t - run_t))
    keep[...] = jnp.exp(-unit * total_t)
    mix_end = (to_end_t * mix_t).astype(bf16)
    cot_dec = (decayed_t * cot_t).astype(bf16)
    ends[...] = dot(mix_end, inject)
    starts[...] = dot(cot_dec, readout)

    part = width // CHUNKS

    def chain(first, last, target, arrive, own, sent, send_sem, recv_sem):
        for c in range(CHUNKS):
            at = pl.ds(c * part, part)
            copy = remote(sent.at[at], arrive.at[at], send_sem.at[c], recv_sem.at[c], d, target)

            @pl.when(jnp.logical_not(first))
            def _():
                copy.wait_recv()

            @pl.when(first)
            def _():
                arrive[at] = jnp.zeros((part, state), f32)

            @pl.when(jnp.logical_not(last))
            def _():
                sent[at] = keep[at] * arrive[at] + own[at]
                copy.start()

    def forward():
        chain(i == 0, i == tm - 1, lax.rem(i + 1, tm), carry, ends, sent_f, f_s, f_r)

    def backward():
        chain(i == tm - 1, i == 0, lax.rem(i + tm - 1, tm), adj, starts, sent_b, b_s, b_r)

    lower = i < tm // 2
    middle = jnp.logical_or(i == tm // 2 - 1, i == tm // 2)
    low_early = jnp.logical_and(lower, jnp.logical_not(middle))
    high_early = jnp.logical_and(jnp.logical_not(lower), jnp.logical_not(middle))
    pl.when(low_early)(forward)
    pl.when(high_early)(backward)

    scores = dot(readout, inject, 1, 1)
    cot_tb = cot_t.astype(bf16)
    pairs = jnp.zeros((frames, frames), f32)
    for h in range(heads):
        cols = slice(h * head, (h + 1) * head)
        gap = run[:, h * head:h * head + 1] - run_t[h * head:h * head + 1, :]
        decay = jnp.where(causal, jnp.exp(-unit * gap), 0.0)
        mixing = (decay * scores).astype(bf16)
        ylocal[:, cols] = dot(mixing, mix[:, cols])
        pairs = pairs + decay * dot(og[:, cols], mix[:, cols], 1, 1)
        glocal[cols, :] = dot(cot_tb[cols, :], mixing)
    pairs = pairs.astype(bf16)
    inj_local = dot(proj_t[state:], pairs)
    read_local = dot(proj_t[:state], pairs, 1, 1)

    pl.when(jnp.logical_and(lower, middle))(forward)
    pl.when(jnp.logical_not(high_early))(backward)
    pl.when(jnp.logical_not(lower))(forward)

    adj_b = adj[...].astype(bf16)
    carry_b = carry[...].astype(bf16)
    mixer_grad = to_end_t * dot(adj_b, inject, 1, 1) + glocal[...]
    inj_grad = inj_local + dot(adj_b, mix_end, 0, 0)
    read_grad = read_local + dot(carry_b, cot_dec, 0, 0)

    def rounded(a):
        return (scale * a).astype(bf16).astype(f32)

    gt[0:width] = rounded(mixer_grad)
    gt[width:width + state] = rounded(inj_grad)
    gt[width + state:width + 2 * state] = rounded(read_grad)

    g_copies = []
    for q in range(PIECES):
        for k in range(1, groups):
            to = lax.rem(d + k, groups)
            at = pl.ds(pl.multiple_of(to * block + q * piece, 8), piece)
            copy = remote(gt.at[at], gall.at[d, q], g_s.at[q, k], g_r.at[q, k], to, i)
            copy.start()
            g_copies.append(copy)
        gall[d, q] = gt[pl.ds(pl.multiple_of(d * block + q * piece, 8), piece)]
    y_ref[...] = (
        jnp.exp(-unit * run) * dot(readout, carry_b, 1, 1) + ylocal[...]
    ).astype(bf16)
    for copy in rec_copies:
        copy.wait_recv()
    for r in range(groups):
        rhs[r * frames:(r + 1) * frames] = rec_all[r].astype(bf16)

    c_copies, z_copies, o_copies = [], [], []

    def product(q):
        for copy in g_copies[q * (groups - 1):(q + 1) * (groups - 1)]:
            copy.wait_recv()
        lhs = jnp.concatenate([gall[r, q].astype(bf16) for r in range(groups)], axis=1)
        for zt in range(chips):
            prod = dot(lhs, rhs[:, zt * 2 * rows:(zt + 1) * 2 * rows])
            pt[0, q, zt] = prod[:, :rows]
            pt[1, q, zt] = prod[:, rows:]
        copy = remote(pt.at[1 - core, q], pbuf.at[q], c_s.at[q], c_r.at[q], d, partner)
        copy.start()
        c_copies.append(copy)

    def over_chips(q):
        c_copies[q].wait_recv()
        for k in range(1, chips):
            zt = lax.rem(z + k, chips)
            qs[q, k] = pt[core, q, zt] + pbuf[q, zt]
            copy = remote(qs.at[q, k], rbuf.at[q, k], z_s.at[q, k], z_r.at[q, k], d, zt * 2 + core)
            copy.start()
            z_copies.append(copy)

    def over_groups(q):
        total = pt[core, q, z] + pbuf[q, z]
        for k in range(1, chips):
            z_copies[q * (chips - 1) + k - 1].wait_recv()
            total = total + rbuf[q, k]
        fin[d, q] = total
        for k in range(1, groups):
            copy = remote(fin.at[d, q], fin.at[d, q], o_s.at[q, k], o_r.at[q, k],
                          lax.rem(d + k, groups), i)
            copy.start()
            o_copies.append(copy)

    for step in range(PIECES + 2):
        if step < PIECES:
            product(step)
        if 1 <= step <= PIECES:
            over_chips(step - 1)
        if step >= 2:
            over_groups(step - 2)
    for copy in o_copies:
        copy.wait_recv()
    out_ref[...] = fin[...]

    for copy in rec_copies + g_copies + c_copies + z_copies + o_copies:
        copy.wait_send()

    for c in range(CHUNKS):
        at = pl.ds(c * part, part)

        @pl.when(i < tm - 1)
        def _():
            remote(sent_f.at[at], carry.at[at], f_s.at[c], f_r.at[c], d, lax.rem(i + 1, tm)).wait_send()

        @pl.when(i > 0)
        def _():
            remote(sent_b.at[at], adj.at[at], b_s.at[c], b_r.at[c], d, lax.rem(i + tm - 1, tm)).wait_send()


def body(records, x_weight, bc_weight, decay_codes, out_grad):
    signal = records[0]
    codes = decay_codes[0].T
    frames, model = signal.shape
    width = x_weight.shape[1]
    wide = width + bc_weight.shape[1]
    state = bc_weight.shape[1] // 2
    tm = lax.axis_size("tm")
    groups = lax.axis_size("dp")
    chips = tm // 2
    rows = model // tm
    piece = wide // groups // PIECES
    grad_scale = (groups * frames * tm) ** (-0.5)
    vmem = pl.BlockSpec(memory_space=pltpu.VMEM)

    def buf(*shape):
        return pltpu.VMEM(shape, f32)

    def sems(*n):
        return [pltpu.SemaphoreType.DMA(n), pltpu.SemaphoreType.DMA(n)]

    y, out = pl.pallas_call(
        functools.partial(kernel, groups, tm),
        out_shape=(
            jax.ShapeDtypeStruct((frames, width), bf16),
            jax.ShapeDtypeStruct((groups, PIECES, piece, rows), f32),
        ),
        in_specs=[pl.BlockSpec(memory_space=pl.ANY)] * 5,
        out_specs=(vmem, vmem),
        scratch_shapes=[
            pltpu.VMEM((frames, model), bf16), pltpu.VMEM(x_weight.shape, bf16),
            pltpu.VMEM(bc_weight.shape, bf16), pltpu.VMEM(codes.shape, jnp.int32),
            pltpu.VMEM((frames, width), bf16), pltpu.SemaphoreType.DMA((5,)),
            buf(groups, frames, model), pltpu.VMEM((groups * frames, model), bf16),
            buf(width, state), buf(width, state), buf(width, state), buf(width, state),
            buf(width, state), buf(width, state), buf(width, state),
            buf(wide, frames), buf(groups, PIECES, piece, frames),
            buf(2, PIECES, chips, piece, rows), buf(PIECES, chips, piece, rows),
            buf(PIECES, chips, piece, rows), buf(PIECES, chips, piece, rows),
            buf(groups, PIECES, piece, rows), buf(frames, width), buf(width, frames),
            *sems(groups), *sems(CHUNKS), *sems(CHUNKS), *sems(PIECES, groups),
            *sems(PIECES), *sems(PIECES, chips), *sems(PIECES, groups),
        ],
        compiler_params=pltpu.CompilerParams(
            collective_id=0, has_side_effects=True, vmem_limit_bytes=60 * 1024 * 1024
        ),
    )(signal, x_weight, bc_weight, codes, out_grad[0])
    out = out.reshape(wide, rows).T * grad_scale
    return (y[None], out[:, :width], out[:, width:])


def solution(mesh):
    return jax.shard_map(
        body,
        mesh=mesh,
        in_specs=(P("dp", "tm", None), P(), P(), P("dp", "tm", None), P("dp", "tm", None)),
        out_specs=(P("dp", "tm", None), P("tm", None), P("tm", None)),
        check_vma=False,
    )
```

```python
import functools

import jax
import jax.numpy as jnp
from jax import lax
from jax.experimental import pallas as pl
from jax.experimental.pallas import tpu as pltpu
from jax.sharding import PartitionSpec as P

MESH = pl.DeviceIdType.MESH
CHUNKS = 4
PIECES = 3
f32 = jnp.float32
bf16 = jnp.bfloat16


def dot(a, b, left=1, right=0):
    return lax.dot_general(
        a, b, (((left,), (right,)), ((), ())), preferred_element_type=f32
    )


def kernel(
    groups, tm, rec_hbm, xw_hbm, bw_hbm, code_hbm, og_hbm, y_ref, x_out, bc_out,
    rec_ref, xw_ref, bw_ref, code_ref, og_ref, in_s, rec_all, rhs, own, give, given, give_d, given_d, hop_in, hop_out, entering, passed,
    gt, gall, pt, pbuf, qs, rbuf, fin, ylocal, glocal,
    rec_s, rec_r, e_s, e_r, h_s, h_r, p_s, p_r, g_s, g_r, c_s, c_r, z_s, z_r, o_s, o_r,
):
    heads, frames = code_ref.shape
    width = xw_ref.shape[1]
    head = width // heads
    state = bw_ref.shape[1] // 2
    piece, rows = fin.shape[2:]
    block = PIECES * piece
    chips = tm // 2
    unit = 1.0 / (32.0 * frames * tm)
    scale = (state * frames * tm) ** (-0.5)

    loads = []
    for n, (src, dst) in enumerate((
        (rec_hbm, rec_ref), (bw_hbm, bw_ref), (xw_hbm, xw_ref), (code_hbm, code_ref), (og_hbm, og_ref),
    )):
        load = pltpu.make_async_copy(src, dst, in_s.at[n])
        load.start()
        loads.append(load)

    d = lax.axis_index("dp")
    i = lax.axis_index("tm")
    z = i // 2
    core = i % 2
    partner = i + 1 - 2 * core

    barrier = pltpu.get_barrier_semaphore()

    def greet(dp_to, tm_to):
        pl.semaphore_signal(barrier, inc=1, device_id=(dp_to, tm_to), device_id_type=MESH)

    for k in range(1, groups):
        greet(lax.rem(d + k, groups), i)
    for k in range(1, chips):
        greet(d, lax.rem(z + k, chips) * 2 + core)
    greet(d, partner)

    loads[0].wait()
    rec = rec_ref[...]
    rec_all[d] = rec.astype(f32)
    pl.semaphore_wait(barrier, (groups - 1) + (chips - 1) + 1)

    def remote(src, dst, send, recv, dp_to, tm_to):
        return pltpu.make_async_remote_copy(
            src_ref=src, dst_ref=dst, send_sem=send, recv_sem=recv,
            device_id=(dp_to, tm_to), device_id_type=MESH,
        )

    rec_copies = []

    def send_rec(n, source, half, to):
        size = frames if half is None else frames // 2
        ref = rec_all.at[source, pl.ds((half or 0) * size, size)]
        copy = remote(ref, ref, rec_s.at[n], rec_r.at[n], to, i)
        copy.start()
        rec_copies.append(copy)
        return copy

    square = groups == 4
    if square:
        beside = d + 1 - 2 * (d % 2)
        across = lax.rem(d + 2, groups)
        first_a = send_rec(0, d, 0, beside)
        first_b = send_rec(1, d, 1, across)
        send_rec(2, d, 1, beside)
        send_rec(3, d, 0, across)
    else:
        for k in range(1, groups):
            send_rec(k, d, None, lax.rem(d + k, groups))

    for load in loads[1:]:
        load.wait()
    mix = dot(rec, xw_ref[...]).astype(bf16)
    proj = dot(rec, bw_ref[...]).astype(bf16)
    inject, readout = proj[:, :state], proj[:, state:]
    og = og_ref[...]
    mix_t = mix.astype(f32).T
    cot_t = og.astype(f32).T
    proj_t = proj.astype(f32).T.astype(bf16)

    codes = code_ref[...].astype(f32)
    high = jnp.floor(codes * 0.125)
    low = codes - 8.0 * high
    spread = (
        lax.broadcasted_iota(jnp.int32, (heads, width), 1) // head
        == lax.broadcasted_iota(jnp.int32, (heads, width), 0)
    ).astype(f32)
    high_w, low_w = dot(high, spread, 0, 0), dot(low, spread, 0, 0)
    high_t, low_t = dot(spread, high, 0, 0), dot(spread, low, 0, 0)
    t_at = lax.broadcasted_iota(jnp.int32, (frames, frames), 0)
    s_at = lax.broadcasted_iota(jnp.int32, (frames, frames), 1)
    causal = t_at >= s_at
    tri = causal.astype(f32).astype(bf16)
    upper_tri = (t_at <= s_at).astype(f32).astype(bf16)
    sums = jnp.concatenate([upper_tri, jnp.ones((frames, frames), bf16)], axis=1)
    run = 8.0 * dot(tri, high_w.astype(bf16)) + dot(tri, low_w.astype(bf16))
    both = 8.0 * dot(high_t.astype(bf16), sums) + dot(low_t.astype(bf16), sums)
    run_t, total_t = both[:, :frames], both[:, frames:]
    decayed_t = jnp.exp(-unit * run_t)
    to_end_t = jnp.exp(-unit * (total_t - run_t))
    mix_end = (to_end_t * mix_t).astype(bf16)
    cot_dec = (decayed_t * cot_t).astype(bf16)
    ones = jnp.ones((frames, 128), f32)
    give_d[...] = jnp.exp(-unit * (8.0 * dot(high, ones) + dot(low, ones)))
    ends = dot(mix_end, inject)
    starts = dot(cot_dec, readout)

    forward = core == 1

    @pl.when(forward)
    def _():
        own[...] = ends
        give[...] = starts

    @pl.when(jnp.logical_not(forward))
    def _():
        own[...] = starts
        give[...] = ends

    part = width // CHUNKS
    per = heads // CHUNKS
    place = jnp.where(forward, z, chips - 1 - z)
    onward = lax.rem(jnp.where(forward, z + 1, z + chips - 1), chips) * 2 + core
    exchange = [remote(give_d, given_d, e_s.at[CHUNKS], e_r.at[CHUNKS], d, partner)]
    hops, passes = [], []
    for c in range(CHUNKS):
        at = pl.ds(c * part, part)
        exchange.append(remote(give.at[at], given.at[at], e_s.at[c], e_r.at[c], d, partner))
        hops.append(remote(hop_out.at[at], hop_in.at[at], h_s.at[c], h_r.at[c], d, onward))
        passes.append(remote(hop_in.at[at], passed.at[at], p_s.at[c], p_r.at[c], d, partner))
    for copy in exchange:
        copy.start()

    def chain():
        exchange[0].wait_recv()

        def factors(ref, c):
            return jnp.concatenate(
                [jnp.broadcast_to(ref[h:h + 1, :], (head, 128)) for h in range(c * per, (c + 1) * per)],
                axis=0,
            )

        for c in range(CHUNKS):
            at = pl.ds(c * part, part)
            exchange[c + 1].wait_recv()

            @pl.when(place > 0)
            def _():
                hops[c].wait_recv()

            @pl.when(place == 0)
            def _():
                hop_in[at] = jnp.zeros((part, state), f32)

            inside = factors(given_d, c) * hop_in[at] + given[at]
            entering[at] = inside

            @pl.when(place < chips - 1)
            def _():
                hop_out[at] = factors(give_d, c) * inside + own[at]
                hops[c].start()

            passes[c].start()

    early = place < chips // 2
    pl.when(early)(chain)

    scores = dot(readout, inject, 1, 1)
    cot_tb = cot_t.astype(bf16)
    pairs = jnp.zeros((frames, frames), f32)
    for h in range(heads):
        cols = slice(h * head, (h + 1) * head)
        gap = run[:, h * head:h * head + 1] - run_t[h * head:h * head + 1, :]
        decay = jnp.where(causal, jnp.exp(-unit * gap), 0.0)
        mixing = (decay * scores).astype(bf16)
        ylocal[:, cols] = dot(mixing, mix[:, cols])
        pairs = pairs + decay * dot(og[:, cols], mix[:, cols], 1, 1)
        glocal[cols, :] = dot(cot_tb[cols, :], mixing)
    pairs = pairs.astype(bf16)
    inj_local = dot(proj_t[state:], pairs)
    read_local = dot(proj_t[:state], pairs, 1, 1)

    if square:
        first_a.wait_recv()
        send_rec(4, beside, 0, across)
        first_b.wait_recv()
        send_rec(5, across, 1, beside)

    pl.when(jnp.logical_not(early))(chain)
    for copy in passes:
        copy.wait_recv()

    mine, theirs = entering[...].astype(bf16), passed[...].astype(bf16)
    carry_b = jnp.where(forward, mine, theirs)
    adj_b = jnp.where(forward, theirs, mine)
    mixer_grad = to_end_t * dot(adj_b, inject, 1, 1) + glocal[...]
    inj_grad = inj_local + dot(adj_b, mix_end, 0, 0)
    read_grad = read_local + dot(carry_b, cot_dec, 0, 0)

    def rounded(a):
        return (scale * a).astype(bf16).astype(f32)

    gt[0:width] = rounded(mixer_grad)
    gt[width:width + state] = rounded(inj_grad)
    gt[width + state:width + 2 * state] = rounded(read_grad)

    g_copies = []
    for q in range(PIECES):
        for k in range(1, groups):
            to = lax.rem(d + k, groups)
            at = pl.ds(pl.multiple_of(to * block + q * piece, 8), piece)
            copy = remote(gt.at[at], gall.at[d, q], g_s.at[q, k], g_r.at[q, k], to, i)
            copy.start()
            g_copies.append(copy)
        gall[d, q] = gt[pl.ds(pl.multiple_of(d * block + q * piece, 8), piece)]
    y_ref[...] = (
        jnp.exp(-unit * run) * dot(readout, carry_b, 1, 1) + ylocal[...]
    ).astype(bf16)
    for copy in rec_copies:
        if not (square and (copy is first_a or copy is first_b)):
            copy.wait_recv()
    for r in range(groups):
        rhs[r * frames:(r + 1) * frames] = rec_all[r].astype(bf16)

    c_copies, z_copies, o_copies = [], [], []

    def product(q):
        for copy in g_copies[q * (groups - 1):(q + 1) * (groups - 1)]:
            copy.wait_recv()
        lhs = jnp.concatenate([gall[r, q].astype(bf16) for r in range(groups)], axis=1)
        for zt in range(chips):
            prod = dot(lhs, rhs[:, zt * 2 * rows:(zt + 1) * 2 * rows])
            pt[0, q, zt] = prod[:, :rows]
            pt[1, q, zt] = prod[:, rows:]
        copy = remote(pt.at[1 - core, q], pbuf.at[q], c_s.at[q], c_r.at[q], d, partner)
        copy.start()
        c_copies.append(copy)

    def over_chips(q):
        c_copies[q].wait_recv()
        for k in range(1, chips):
            zt = lax.rem(z + k, chips)
            qs[q, k] = pt[core, q, zt] + pbuf[q, zt]
            copy = remote(qs.at[q, k], rbuf.at[q, k], z_s.at[q, k], z_r.at[q, k], d, zt * 2 + core)
            copy.start()
            z_copies.append(copy)

    def over_groups(q):
        total = pt[core, q, z] + pbuf[q, z]
        for k in range(1, chips):
            z_copies[q * (chips - 1) + k - 1].wait_recv()
            total = total + rbuf[q, k]
        fin[d, q] = total
        for k in range(1, groups):
            copy = remote(fin.at[d, q], fin.at[d, q], o_s.at[q, k], o_r.at[q, k],
                          lax.rem(d + k, groups), i)
            copy.start()
            o_copies.append(copy)

    for step in range(PIECES + 2):
        if step < PIECES:
            product(step)
        if 1 <= step <= PIECES:
            over_chips(step - 1)
        if step >= 2:
            over_groups(step - 2)
    for copy in o_copies:
        copy.wait_recv()
    whole = fin[...].reshape(groups * block, rows).T * ((groups * frames * tm) ** (-0.5))
    x_out[...] = whole[:, :width]
    bc_out[...] = whole[:, width:]

    for copy in rec_copies + exchange + passes + g_copies + c_copies + z_copies + o_copies:
        copy.wait_send()
    for copy in hops:
        pl.when(place < chips - 1)(copy.wait_send)


def body(records, x_weight, bc_weight, decay_codes, out_grad):
    signal = records[0]
    codes = decay_codes[0].T
    frames, model = signal.shape
    width = x_weight.shape[1]
    wide = width + bc_weight.shape[1]
    state = bc_weight.shape[1] // 2
    tm = lax.axis_size("tm")
    groups = lax.axis_size("dp")
    chips = tm // 2
    rows = model // tm
    piece = wide // groups // PIECES
    vmem = pl.BlockSpec(memory_space=pltpu.VMEM)

    def buf(*shape):
        return pltpu.VMEM(shape, f32)

    def sems(*n):
        return [pltpu.SemaphoreType.DMA(n), pltpu.SemaphoreType.DMA(n)]

    y, x_grad, bc_grad = pl.pallas_call(
        functools.partial(kernel, groups, tm),
        out_shape=(
            jax.ShapeDtypeStruct((frames, width), bf16),
            jax.ShapeDtypeStruct((rows, width), f32),
            jax.ShapeDtypeStruct((rows, wide - width), f32),
        ),
        in_specs=[pl.BlockSpec(memory_space=pl.ANY)] * 5,
        out_specs=(vmem, vmem, vmem),
        scratch_shapes=[
            pltpu.VMEM((frames, model), bf16), pltpu.VMEM(x_weight.shape, bf16),
            pltpu.VMEM(bc_weight.shape, bf16), pltpu.VMEM(codes.shape, jnp.int32),
            pltpu.VMEM((frames, width), bf16), pltpu.SemaphoreType.DMA((5,)),
            buf(groups, frames, model), pltpu.VMEM((groups * frames, model), bf16),
            buf(width, state), buf(width, state), buf(width, state),
            buf(codes.shape[0], 128), buf(codes.shape[0], 128),
            buf(width, state), buf(width, state), buf(width, state), buf(width, state),
            buf(wide, frames), buf(groups, PIECES, piece, frames),
            buf(2, PIECES, chips, piece, rows), buf(PIECES, chips, piece, rows),
            buf(PIECES, chips, piece, rows), buf(PIECES, chips, piece, rows),
            buf(groups, PIECES, piece, rows), buf(frames, width), buf(width, frames),
            *sems(max(groups, 6)), *sems(CHUNKS + 1), *sems(CHUNKS), *sems(CHUNKS), *sems(PIECES, groups),
            *sems(PIECES), *sems(PIECES, chips), *sems(PIECES, groups),
        ],
        compiler_params=pltpu.CompilerParams(
            collective_id=0, has_side_effects=True, vmem_limit_bytes=60 * 1024 * 1024
        ),
    )(signal, x_weight, bc_weight, codes, out_grad[0])
    return (y[None], x_grad, bc_grad)


def solution(mesh):
    return jax.shard_map(
        body,
        mesh=mesh,
        in_specs=(P("dp", "tm", None), P(), P(), P("dp", "tm", None), P("dp", "tm", None)),
        out_specs=(P("dp", "tm", None), P("tm", None), P("tm", None)),
        check_vma=False,
    )
```

```python
import functools

import jax
import jax.numpy as jnp
from jax import lax
from jax.experimental import pallas as pl
from jax.experimental.pallas import tpu as pltpu
from jax.sharding import PartitionSpec as P

MESH = pl.DeviceIdType.MESH
CHUNKS = 8
PIECES = 3
f32 = jnp.float32
bf16 = jnp.bfloat16


def dot(a, b, left=1, right=0):
    return lax.dot_general(
        a, b, (((left,), (right,)), ((), ())), preferred_element_type=f32
    )


def kernel(
    groups, tm, rec_hbm, xw_hbm, bw_hbm, code_hbm, og_hbm, y_ref, x_out, bc_out,
    rec_ref, xw_ref, bw_ref, code_ref, og_ref, in_s, rec_all, rhs, own, give, given, give_d, given_d, hop_in, hop_out, entering, passed,
    gt, gall, pt, pbuf, qs, rbuf, fin, ylocal, glocal,
    rec_s, rec_r, e_s, e_r, h_s, h_r, p_s, p_r, g_s, g_r, c_s, c_r, z_s, z_r, o_s, o_r,
):
    heads, frames = code_ref.shape
    width = xw_ref.shape[1]
    head = width // heads
    state = bw_ref.shape[1] // 2
    piece, rows = fin.shape[2:]
    block = PIECES * piece
    chips = tm // 2
    unit = 1.0 / (32.0 * frames * tm)
    scale = (state * frames * tm) ** (-0.5)

    loads = []
    for n, (src, dst) in enumerate((
        (rec_hbm, rec_ref), (bw_hbm, bw_ref), (xw_hbm, xw_ref), (code_hbm, code_ref), (og_hbm, og_ref),
    )):
        load = pltpu.make_async_copy(src, dst, in_s.at[n])
        load.start()
        loads.append(load)

    d = lax.axis_index("dp")
    i = lax.axis_index("tm")
    z = i // 2
    core = i % 2
    partner = i + 1 - 2 * core

    barrier = pltpu.get_barrier_semaphore()

    def greet(dp_to, tm_to):
        pl.semaphore_signal(barrier, inc=1, device_id=(dp_to, tm_to), device_id_type=MESH)

    for k in range(1, groups):
        greet(lax.rem(d + k, groups), i)
    for k in range(1, chips):
        greet(d, lax.rem(z + k, chips) * 2 + core)
    greet(d, partner)

    loads[0].wait()
    rec = rec_ref[...]
    rec_all[d] = rec.astype(f32)
    pl.semaphore_wait(barrier, (groups - 1) + (chips - 1) + 1)

    def remote(src, dst, send, recv, dp_to, tm_to):
        return pltpu.make_async_remote_copy(
            src_ref=src, dst_ref=dst, send_sem=send, recv_sem=recv,
            device_id=(dp_to, tm_to), device_id_type=MESH,
        )

    rec_copies = []

    def send_rec(n, source, half, to, start=True):
        size = frames if half is None else frames // 2
        ref = rec_all.at[source, pl.ds((half or 0) * size, size)]
        copy = remote(ref, ref, rec_s.at[n], rec_r.at[n], to, i)
        if start:
            copy.start()
        rec_copies.append(copy)
        return copy

    square = groups == 4
    if square:
        beside = d + 1 - 2 * (d % 2)
        across = lax.rem(d + 2, groups)
        first_a = send_rec(0, d, 0, beside)
        first_b = send_rec(1, d, 1, across)
        send_rec(2, d, 1, beside)
        send_rec(3, d, 0, across)
        relay_a = send_rec(4, beside, 0, across, False)
        relay_b = send_rec(5, across, 1, beside, False)
    else:
        for k in range(1, groups):
            send_rec(k, d, None, lax.rem(d + k, groups))

    for load in loads[1:]:
        load.wait()
    mix = dot(rec, xw_ref[...]).astype(bf16)
    proj = dot(rec, bw_ref[...]).astype(bf16)
    inject, readout = proj[:, :state], proj[:, state:]
    og = og_ref[...]
    mix_t = mix.astype(f32).T
    cot_t = og.astype(f32).T
    proj_t = proj.astype(f32).T.astype(bf16)

    codes = code_ref[...].astype(f32)
    high = jnp.floor(codes * 0.125)
    low = codes - 8.0 * high
    spread = (
        lax.broadcasted_iota(jnp.int32, (heads, width), 1) // head
        == lax.broadcasted_iota(jnp.int32, (heads, width), 0)
    ).astype(f32)
    high_w, low_w = dot(high, spread, 0, 0), dot(low, spread, 0, 0)
    high_t, low_t = dot(spread, high, 0, 0), dot(spread, low, 0, 0)
    t_at = lax.broadcasted_iota(jnp.int32, (frames, frames), 0)
    s_at = lax.broadcasted_iota(jnp.int32, (frames, frames), 1)
    causal = t_at >= s_at
    tri = causal.astype(f32).astype(bf16)
    upper_tri = (t_at <= s_at).astype(f32).astype(bf16)
    sums = jnp.concatenate([upper_tri, jnp.ones((frames, frames), bf16)], axis=1)
    run = 8.0 * dot(tri, high_w.astype(bf16)) + dot(tri, low_w.astype(bf16))
    both = 8.0 * dot(high_t.astype(bf16), sums) + dot(low_t.astype(bf16), sums)
    run_t, total_t = both[:, :frames], both[:, frames:]
    decayed_t = jnp.exp(-unit * run_t)
    to_end_t = jnp.exp(-unit * (total_t - run_t))
    mix_end = (to_end_t * mix_t).astype(bf16)
    cot_dec = (decayed_t * cot_t).astype(bf16)
    ones = jnp.ones((frames, 128), f32)
    give_d[...] = jnp.exp(-unit * (8.0 * dot(high, ones) + dot(low, ones)))
    ends = dot(mix_end, inject)
    starts = dot(cot_dec, readout)

    forward = core == 1

    @pl.when(forward)
    def _():
        own[...] = ends
        give[...] = starts

    @pl.when(jnp.logical_not(forward))
    def _():
        own[...] = starts
        give[...] = ends

    part = width // CHUNKS
    per = heads // CHUNKS
    place = jnp.where(forward, z, chips - 1 - z)
    onward = lax.rem(jnp.where(forward, z + 1, z + chips - 1), chips) * 2 + core
    exchange = [remote(give_d, given_d, e_s.at[CHUNKS], e_r.at[CHUNKS], d, partner)]
    hops, passes = [], []
    for c in range(CHUNKS):
        at = pl.ds(c * part, part)
        exchange.append(remote(give.at[at], given.at[at], e_s.at[c], e_r.at[c], d, partner))
        hops.append(remote(hop_out.at[at], hop_in.at[at], h_s.at[c], h_r.at[c], d, onward))
        passes.append(remote(hop_in.at[at], passed.at[at], p_s.at[c], p_r.at[c], d, partner))
    for copy in exchange:
        copy.start()

    def chain(chunks):
        if chunks[0] == 0:
            exchange[0].wait_recv()

        def factors(ref, c):
            return jnp.concatenate(
                [jnp.broadcast_to(ref[h:h + 1, :], (head, 128)) for h in range(c * per, (c + 1) * per)],
                axis=0,
            )

        for c in chunks:
            at = pl.ds(c * part, part)
            exchange[c + 1].wait_recv()

            @pl.when(place > 0)
            def _():
                hops[c].wait_recv()

            @pl.when(place == 0)
            def _():
                hop_in[at] = jnp.zeros((part, state), f32)

            inside = factors(given_d, c) * hop_in[at] + given[at]
            entering[at] = inside

            @pl.when(place < chips - 1)
            def _():
                hop_out[at] = factors(give_d, c) * inside + own[at]
                hops[c].start()

            passes[c].start()

    early = place < chips // 2
    late = jnp.logical_not(early)

    def relay():
        if square:
            first_a.wait_recv()
            relay_a.start()
            first_b.wait_recv()
            relay_b.start()

    @pl.when(early)
    def _():
        chain(range(CHUNKS))
        relay()

    scores = dot(readout, inject, 1, 1)
    cot_tb = cot_t.astype(bf16)
    pairs = jnp.zeros((frames, frames), f32)
    for h in range(heads):
        cols = slice(h * head, (h + 1) * head)
        gap = run[:, h * head:h * head + 1] - run_t[h * head:h * head + 1, :]
        decay = jnp.where(causal, jnp.exp(-unit * gap), 0.0)
        mixing = (decay * scores).astype(bf16)
        ylocal[:, cols] = dot(mixing, mix[:, cols])
        pairs = pairs + decay * dot(og[:, cols], mix[:, cols], 1, 1)
        glocal[cols, :] = dot(cot_tb[cols, :], mixing)
    pairs = pairs.astype(bf16)
    inj_local = dot(proj_t[state:], pairs)
    read_local = dot(proj_t[:state], pairs, 1, 1)

    pl.when(late)(relay)

    def rounded(a):
        return (scale * a).astype(bf16).astype(f32)

    g_copies = []

    def send_g(q):
        for k in range(1, groups):
            to = lax.rem(d + k, groups)
            at = pl.ds(pl.multiple_of((q * groups + to) * piece, 8), piece)
            copy = remote(gt.at[at], gall.at[d, q], g_s.at[q, k], g_r.at[q, k], to, i)
            copy.start()
            g_copies.append(copy)
        gall[d, q] = gt[pl.ds(pl.multiple_of((q * groups + d) * piece, 8), piece)]

    split = groups * piece
    adjs, carries = [], []
    for q in range(PIECES - 1):
        at = slice(q * split, (q + 1) * split)
        chunks = range(q * split // part, (q + 1) * split // part)
        pl.when(late)(functools.partial(chain, chunks))
        for c in chunks:
            passes[c].wait_recv()
        mine, theirs = entering[at].astype(bf16), passed[at].astype(bf16)
        adjs.append(jnp.where(forward, theirs, mine))
        carries.append(jnp.where(forward, mine, theirs))
        gt[at] = rounded(to_end_t[at] * dot(adjs[q], inject, 1, 1) + glocal[at])
        send_g(q)
    adj_b = jnp.concatenate(adjs, axis=0)
    carry_b = jnp.concatenate(carries, axis=0)
    inj_grad = inj_local + dot(adj_b, mix_end, 0, 0)
    read_grad = read_local + dot(carry_b, cot_dec, 0, 0)
    gt[width:width + state] = rounded(inj_grad)
    gt[width + state:width + 2 * state] = rounded(read_grad)
    send_g(PIECES - 1)
    y_ref[...] = (
        jnp.exp(-unit * run) * dot(readout, carry_b, 1, 1) + ylocal[...]
    ).astype(bf16)
    for copy in rec_copies:
        if not (square and (copy is first_a or copy is first_b)):
            copy.wait_recv()
    for r in range(groups):
        rhs[r * frames:(r + 1) * frames] = rec_all[r].astype(bf16)

    c_copies, z_copies, o_copies = [], [], []

    def product(q):
        for copy in g_copies[q * (groups - 1):(q + 1) * (groups - 1)]:
            copy.wait_recv()
        lhs = jnp.concatenate([gall[r, q].astype(bf16) for r in range(groups)], axis=1)
        for zt in range(chips):
            prod = dot(lhs, rhs[:, zt * 2 * rows:(zt + 1) * 2 * rows])
            pt[0, q, zt] = prod[:, :rows]
            pt[1, q, zt] = prod[:, rows:]
        copy = remote(pt.at[1 - core, q], pbuf.at[q], c_s.at[q], c_r.at[q], d, partner)
        copy.start()
        c_copies.append(copy)

    def over_chips(q):
        c_copies[q].wait_recv()
        for k in range(1, chips):
            zt = lax.rem(z + k, chips)
            qs[q, k] = pt[core, q, zt] + pbuf[q, zt]
            copy = remote(qs.at[q, k], rbuf.at[q, k], z_s.at[q, k], z_r.at[q, k], d, zt * 2 + core)
            copy.start()
            z_copies.append(copy)

    def over_groups(q):
        total = pt[core, q, z] + pbuf[q, z]
        for k in range(1, chips):
            z_copies[q * (chips - 1) + k - 1].wait_recv()
            total = total + rbuf[q, k]
        fin[q, d] = total
        for k in range(1, groups):
            copy = remote(fin.at[q, d], fin.at[q, d], o_s.at[q, k], o_r.at[q, k],
                          lax.rem(d + k, groups), i)
            copy.start()
            o_copies.append(copy)

    for step in range(PIECES + 2):
        if step < PIECES:
            product(step)
        if 1 <= step <= PIECES:
            over_chips(step - 1)
        if step >= 2:
            over_groups(step - 2)
    for copy in o_copies:
        copy.wait_recv()
    whole = fin[...].reshape(groups * block, rows).T * ((groups * frames * tm) ** (-0.5))
    x_out[...] = whole[:, :width]
    bc_out[...] = whole[:, width:]

    for copy in rec_copies + exchange + passes + g_copies + c_copies + z_copies + o_copies:
        copy.wait_send()
    for copy in hops:
        pl.when(place < chips - 1)(copy.wait_send)


def body(records, x_weight, bc_weight, decay_codes, out_grad):
    signal = records[0]
    codes = decay_codes[0].T
    frames, model = signal.shape
    width = x_weight.shape[1]
    wide = width + bc_weight.shape[1]
    state = bc_weight.shape[1] // 2
    tm = lax.axis_size("tm")
    groups = lax.axis_size("dp")
    chips = tm // 2
    rows = model // tm
    piece = wide // groups // PIECES
    vmem = pl.BlockSpec(memory_space=pltpu.VMEM)

    def buf(*shape):
        return pltpu.VMEM(shape, f32)

    def sems(*n):
        return [pltpu.SemaphoreType.DMA(n), pltpu.SemaphoreType.DMA(n)]

    y, x_grad, bc_grad = pl.pallas_call(
        functools.partial(kernel, groups, tm),
        out_shape=(
            pltpu.VMEM((frames, width), bf16),
            pltpu.VMEM((rows, width), f32),
            pltpu.VMEM((rows, wide - width), f32),
        ),
        in_specs=[pl.BlockSpec(memory_space=pltpu.HBM)] * 5,
        out_specs=(vmem, vmem, vmem),
        scratch_shapes=[
            pltpu.VMEM((frames, model), bf16), pltpu.VMEM(x_weight.shape, bf16),
            pltpu.VMEM(bc_weight.shape, bf16), pltpu.VMEM(codes.shape, jnp.int32),
            pltpu.VMEM((frames, width), bf16), pltpu.SemaphoreType.DMA((5,)),
            buf(groups, frames, model), pltpu.VMEM((groups * frames, model), bf16),
            buf(width, state), buf(width, state), buf(width, state),
            buf(codes.shape[0], 128), buf(codes.shape[0], 128),
            buf(width, state), buf(width, state), buf(width, state), buf(width, state),
            buf(wide, frames), buf(groups, PIECES, piece, frames),
            buf(2, PIECES, chips, piece, rows), buf(PIECES, chips, piece, rows),
            buf(PIECES, chips, piece, rows), buf(PIECES, chips, piece, rows),
            buf(PIECES, groups, piece, rows), buf(frames, width), buf(width, frames),
            *sems(max(groups, 6)), *sems(CHUNKS + 1), *sems(CHUNKS), *sems(CHUNKS), *sems(PIECES, groups),
            *sems(PIECES), *sems(PIECES, chips), *sems(PIECES, groups),
        ],
        compiler_params=pltpu.CompilerParams(
            collective_id=0, has_side_effects=True, vmem_limit_bytes=60 * 1024 * 1024
        ),
    )(signal, x_weight, bc_weight, codes, out_grad[0])
    return (y[None], x_grad, bc_grad)


def solution(mesh):
    return jax.shard_map(
        body,
        mesh=mesh,
        in_specs=(P("dp", "tm", None), P(), P(), P("dp", "tm", None), P("dp", "tm", None)),
        out_specs=(P("dp", "tm", None), P("tm", None), P("tm", None)),
        check_vma=False,
    )
```

```python
import functools

import jax
import jax.numpy as jnp
from jax import lax
from jax.experimental import pallas as pl
from jax.experimental.pallas import tpu as pltpu
from jax.sharding import PartitionSpec as P

MESH = pl.DeviceIdType.MESH
CHUNKS = 8
PIECES = 3
f32 = jnp.float32
bf16 = jnp.bfloat16


def dot(a, b, left=1, right=0):
    return lax.dot_general(
        a, b, (((left,), (right,)), ((), ())), preferred_element_type=f32
    )


def kernel(
    groups, tm, rec_hbm, xw_hbm, bw_hbm, code_hbm, og_hbm, y_ref, x_out, bc_out,
    rec_ref, xw_ref, bw_ref, code_ref, og_ref, in_s, rec_all, rhs, own, give, given, give_d, given_d, hop_in, hop_out, entering, passed,
    gt, gall, pt, pbuf, qs, rbuf, fin, ylocal, glocal,
    rec_s, rec_r, e_s, e_r, h_s, h_r, p_s, p_r, g_s, g_r, c_s, c_r, z_s, z_r, o_s, o_r,
):
    heads, frames = code_ref.shape
    width = xw_ref.shape[1]
    head = width // heads
    state = bw_ref.shape[1] // 2
    piece, rows = fin.shape[2:]
    block = PIECES * piece
    chips = tm // 2
    unit = 1.0 / (32.0 * frames * tm)
    scale = (state * frames * tm) ** (-0.5)

    loads = []
    for n, (src, dst) in enumerate((
        (rec_hbm, rec_ref), (bw_hbm, bw_ref), (xw_hbm, xw_ref), (code_hbm, code_ref), (og_hbm, og_ref),
    )):
        load = pltpu.make_async_copy(src, dst, in_s.at[n])
        load.start()
        loads.append(load)

    d = lax.axis_index("dp")
    i = lax.axis_index("tm")
    z = i // 2
    core = i % 2
    partner = i + 1 - 2 * core

    barrier = pltpu.get_barrier_semaphore()

    def greet(dp_to, tm_to):
        pl.semaphore_signal(barrier, inc=1, device_id=(dp_to, tm_to), device_id_type=MESH)

    for k in range(1, groups):
        greet(lax.rem(d + k, groups), i)
    for k in range(1, chips):
        greet(d, lax.rem(z + k, chips) * 2 + core)
    greet(d, partner)

    loads[0].wait()
    rec = rec_ref[...]
    rec_all[d] = rec.astype(f32)
    pl.semaphore_wait(barrier, (groups - 1) + (chips - 1) + 1)

    def remote(src, dst, send, recv, dp_to, tm_to):
        return pltpu.make_async_remote_copy(
            src_ref=src, dst_ref=dst, send_sem=send, recv_sem=recv,
            device_id=(dp_to, tm_to), device_id_type=MESH,
        )

    rec_copies = []

    def send_rec(n, source, half, to, start=True):
        size = frames if half is None else frames // 2
        ref = rec_all.at[source, pl.ds((half or 0) * size, size)]
        copy = remote(ref, ref, rec_s.at[n], rec_r.at[n], to, i)
        if start:
            copy.start()
        rec_copies.append(copy)
        return copy

    square = groups == 4
    if square:
        beside = d + 1 - 2 * (d % 2)
        across = lax.rem(d + 2, groups)
        first_a = send_rec(0, d, 0, beside)
        first_b = send_rec(1, d, 1, across)
        second_b = send_rec(2, d, 1, beside, False)
        second_a = send_rec(3, d, 0, across, False)
        relay_a = send_rec(4, beside, 0, across, False)
        relay_b = send_rec(5, across, 1, beside, False)
    else:
        for k in range(1, groups):
            send_rec(k, d, None, lax.rem(d + k, groups))

    for load in loads[1:]:
        load.wait()
    mix = dot(rec, xw_ref[...]).astype(bf16)
    proj = dot(rec, bw_ref[...]).astype(bf16)
    inject, readout = proj[:, :state], proj[:, state:]
    og = og_ref[...]
    mix_t = mix.astype(f32).T
    cot_t = og.astype(f32).T
    proj_t = proj.astype(f32).T.astype(bf16)

    codes = code_ref[...].astype(f32)
    high = jnp.floor(codes * 0.125)
    low = codes - 8.0 * high
    spread = (
        lax.broadcasted_iota(jnp.int32, (heads, width), 1) // head
        == lax.broadcasted_iota(jnp.int32, (heads, width), 0)
    ).astype(f32)
    high_w, low_w = dot(high, spread, 0, 0), dot(low, spread, 0, 0)
    high_t, low_t = dot(spread, high, 0, 0), dot(spread, low, 0, 0)
    t_at = lax.broadcasted_iota(jnp.int32, (frames, frames), 0)
    s_at = lax.broadcasted_iota(jnp.int32, (frames, frames), 1)
    causal = t_at >= s_at
    tri = causal.astype(f32).astype(bf16)
    upper_tri = (t_at <= s_at).astype(f32).astype(bf16)
    sums = jnp.concatenate([upper_tri, jnp.ones((frames, frames), bf16)], axis=1)
    run = 8.0 * dot(tri, high_w.astype(bf16)) + dot(tri, low_w.astype(bf16))
    both = 8.0 * dot(high_t.astype(bf16), sums) + dot(low_t.astype(bf16), sums)
    run_t, total_t = both[:, :frames], both[:, frames:]
    decayed_t = jnp.exp(-unit * run_t)
    to_end_t = jnp.exp(-unit * (total_t - run_t))
    mix_end = (to_end_t * mix_t).astype(bf16)
    cot_dec = (decayed_t * cot_t).astype(bf16)
    ones = jnp.ones((frames, 128), f32)
    give_d[...] = jnp.exp(-unit * (8.0 * dot(high, ones) + dot(low, ones)))
    ends = dot(mix_end, inject)
    starts = dot(cot_dec, readout)

    forward = core == 1

    @pl.when(forward)
    def _():
        own[...] = ends
        give[...] = starts

    @pl.when(jnp.logical_not(forward))
    def _():
        own[...] = starts
        give[...] = ends

    part = width // CHUNKS
    per = heads // CHUNKS
    place = jnp.where(forward, z, chips - 1 - z)
    onward = lax.rem(jnp.where(forward, z + 1, z + chips - 1), chips) * 2 + core
    exchange = [remote(give_d, given_d, e_s.at[CHUNKS], e_r.at[CHUNKS], d, partner)]
    hops, passes = [], []
    for c in range(CHUNKS):
        at = pl.ds(c * part, part)
        exchange.append(remote(give.at[at], given.at[at], e_s.at[c], e_r.at[c], d, partner))
        hops.append(remote(hop_out.at[at], hop_in.at[at], h_s.at[c], h_r.at[c], d, onward))
        passes.append(remote(hop_in.at[at], passed.at[at], p_s.at[c], p_r.at[c], d, partner))
    for copy in exchange:
        copy.start()
    if square:
        second_b.start()
        second_a.start()

    def chain(chunks):
        if chunks[0] == 0:
            exchange[0].wait_recv()

        def factors(ref, c):
            return jnp.concatenate(
                [jnp.broadcast_to(ref[h:h + 1, :], (head, 128)) for h in range(c * per, (c + 1) * per)],
                axis=0,
            )

        for c in chunks:
            at = pl.ds(c * part, part)
            exchange[c + 1].wait_recv()

            @pl.when(place > 0)
            def _():
                hops[c].wait_recv()

            @pl.when(place == 0)
            def _():
                hop_in[at] = jnp.zeros((part, state), f32)

            inside = factors(given_d, c) * hop_in[at] + given[at]
            entering[at] = inside

            @pl.when(place < chips - 1)
            def _():
                hop_out[at] = factors(give_d, c) * inside + own[at]
                hops[c].start()

            passes[c].start()

    early = place < chips // 2
    late = jnp.logical_not(early)

    def relay():
        if square:
            first_a.wait_recv()
            relay_a.start()
            first_b.wait_recv()
            relay_b.start()

    @pl.when(early)
    def _():
        chain(range(CHUNKS))
        relay()

    scores = dot(readout, inject, 1, 1)
    cot_tb = cot_t.astype(bf16)
    pairs = jnp.zeros((frames, frames), f32)
    for h in range(heads):
        cols = slice(h * head, (h + 1) * head)
        gap = run[:, h * head:h * head + 1] - run_t[h * head:h * head + 1, :]
        decay = jnp.where(causal, jnp.exp(-unit * gap), 0.0)
        mixing = (decay * scores).astype(bf16)
        ylocal[:, cols] = dot(mixing, mix[:, cols])
        pairs = pairs + decay * dot(og[:, cols], mix[:, cols], 1, 1)
        glocal[cols, :] = dot(cot_tb[cols, :], mixing)
    pairs = pairs.astype(bf16)
    inj_local = dot(proj_t[state:], pairs)
    read_local = dot(proj_t[:state], pairs, 1, 1)

    pl.when(late)(relay)

    def rounded(a):
        return (scale * a).astype(bf16).astype(f32)

    g_copies = []

    def send_g(q):
        for k in range(1, groups):
            to = lax.rem(d + k, groups)
            at = pl.ds(pl.multiple_of((q * groups + to) * piece, 8), piece)
            copy = remote(gt.at[at], gall.at[d, q], g_s.at[q, k], g_r.at[q, k], to, i)
            copy.start()
            g_copies.append(copy)
        gall[d, q] = gt[pl.ds(pl.multiple_of((q * groups + d) * piece, 8), piece)]

    split = groups * piece
    adjs, carries = [], []
    for q in range(PIECES - 1):
        at = slice(q * split, (q + 1) * split)
        chunks = range(q * split // part, (q + 1) * split // part)
        pl.when(late)(functools.partial(chain, chunks))
        for c in chunks:
            passes[c].wait_recv()
        mine, theirs = entering[at].astype(bf16), passed[at].astype(bf16)
        adjs.append(jnp.where(forward, theirs, mine))
        carries.append(jnp.where(forward, mine, theirs))
        gt[at] = rounded(to_end_t[at] * dot(adjs[q], inject, 1, 1) + glocal[at])
        send_g(q)
    adj_b = jnp.concatenate(adjs, axis=0)
    carry_b = jnp.concatenate(carries, axis=0)
    inj_grad = inj_local + dot(adj_b, mix_end, 0, 0)
    read_grad = read_local + dot(carry_b, cot_dec, 0, 0)
    gt[width:width + state] = rounded(inj_grad)
    gt[width + state:width + 2 * state] = rounded(read_grad)
    send_g(PIECES - 1)
    y_ref[...] = (
        jnp.exp(-unit * run) * dot(readout, carry_b, 1, 1) + ylocal[...]
    ).astype(bf16)
    for copy in rec_copies:
        if not (square and (copy is first_a or copy is first_b)):
            copy.wait_recv()
    for r in range(groups):
        rhs[r * frames:(r + 1) * frames] = rec_all[r].astype(bf16)

    c_copies, z_copies, o_copies = [], [], []

    def product(q):
        for copy in g_copies[q * (groups - 1):(q + 1) * (groups - 1)]:
            copy.wait_recv()
        lhs = jnp.concatenate([gall[r, q].astype(bf16) for r in range(groups)], axis=1)
        for zt in range(chips):
            prod = dot(lhs, rhs[:, zt * 2 * rows:(zt + 1) * 2 * rows])
            pt[0, q, zt] = prod[:, :rows]
            pt[1, q, zt] = prod[:, rows:]
        copy = remote(pt.at[1 - core, q], pbuf.at[q], c_s.at[q], c_r.at[q], d, partner)
        copy.start()
        c_copies.append(copy)

    def over_chips(q):
        c_copies[q].wait_recv()
        for k in range(1, chips):
            zt = lax.rem(z + k, chips)
            qs[q, k] = pt[core, q, zt] + pbuf[q, zt]
            copy = remote(qs.at[q, k], rbuf.at[q, k], z_s.at[q, k], z_r.at[q, k], d, zt * 2 + core)
            copy.start()
            z_copies.append(copy)

    def over_groups(q):
        total = pt[core, q, z] + pbuf[q, z]
        for k in range(1, chips):
            z_copies[q * (chips - 1) + k - 1].wait_recv()
            total = total + rbuf[q, k]
        fin[q, d] = total
        for k in range(1, groups):
            copy = remote(fin.at[q, d], fin.at[q, d], o_s.at[q, k], o_r.at[q, k],
                          lax.rem(d + k, groups), i)
            copy.start()
            o_copies.append(copy)

    for step in range(PIECES + 2):
        if step < PIECES:
            product(step)
        if 1 <= step <= PIECES:
            over_chips(step - 1)
        if step >= 2:
            over_groups(step - 2)
    for copy in o_copies:
        copy.wait_recv()
    whole = fin[...].reshape(groups * block, rows).T * ((groups * frames * tm) ** (-0.5))
    x_out[...] = whole[:, :width]
    bc_out[...] = whole[:, width:]

    for copy in rec_copies + exchange + passes + g_copies + c_copies + z_copies + o_copies:
        copy.wait_send()
    for copy in hops:
        pl.when(place < chips - 1)(copy.wait_send)


def body(records, x_weight, bc_weight, decay_codes, out_grad):
    signal = records[0]
    codes = decay_codes[0].T
    frames, model = signal.shape
    width = x_weight.shape[1]
    wide = width + bc_weight.shape[1]
    state = bc_weight.shape[1] // 2
    tm = lax.axis_size("tm")
    groups = lax.axis_size("dp")
    chips = tm // 2
    rows = model // tm
    piece = wide // groups // PIECES
    vmem = pl.BlockSpec(memory_space=pltpu.VMEM)

    def buf(*shape):
        return pltpu.VMEM(shape, f32)

    def sems(*n):
        return [pltpu.SemaphoreType.DMA(n), pltpu.SemaphoreType.DMA(n)]

    y, x_grad, bc_grad = pl.pallas_call(
        functools.partial(kernel, groups, tm),
        out_shape=(
            pltpu.VMEM((frames, width), bf16),
            pltpu.VMEM((rows, width), f32),
            pltpu.VMEM((rows, wide - width), f32),
        ),
        in_specs=[pl.BlockSpec(memory_space=pltpu.HBM)] * 5,
        out_specs=(vmem, vmem, vmem),
        scratch_shapes=[
            pltpu.VMEM((frames, model), bf16), pltpu.VMEM(x_weight.shape, bf16),
            pltpu.VMEM(bc_weight.shape, bf16), pltpu.VMEM(codes.shape, jnp.int32),
            pltpu.VMEM((frames, width), bf16), pltpu.SemaphoreType.DMA((5,)),
            buf(groups, frames, model), pltpu.VMEM((groups * frames, model), bf16),
            buf(width, state), buf(width, state), buf(width, state),
            buf(codes.shape[0], 128), buf(codes.shape[0], 128),
            buf(width, state), buf(width, state), buf(width, state), buf(width, state),
            buf(wide, frames), buf(groups, PIECES, piece, frames),
            buf(2, PIECES, chips, piece, rows), buf(PIECES, chips, piece, rows),
            buf(PIECES, chips, piece, rows), buf(PIECES, chips, piece, rows),
            buf(PIECES, groups, piece, rows), buf(frames, width), buf(width, frames),
            *sems(max(groups, 6)), *sems(CHUNKS + 1), *sems(CHUNKS), *sems(CHUNKS), *sems(PIECES, groups),
            *sems(PIECES), *sems(PIECES, chips), *sems(PIECES, groups),
        ],
        compiler_params=pltpu.CompilerParams(
            collective_id=0, has_side_effects=True, vmem_limit_bytes=60 * 1024 * 1024
        ),
    )(signal, x_weight, bc_weight, codes, out_grad[0])
    return (y[None], x_grad, bc_grad)


def solution(mesh):
    return jax.shard_map(
        body,
        mesh=mesh,
        in_specs=(P("dp", "tm", None), P(), P(), P("dp", "tm", None), P("dp", "tm", None)),
        out_specs=(P("dp", "tm", None), P("tm", None), P("tm", None)),
        check_vma=False,
    )
```

```python
import functools

import jax
import jax.numpy as jnp
from jax import lax
from jax.experimental import pallas as pl
from jax.experimental.pallas import tpu as pltpu
from jax.sharding import PartitionSpec as P

MESH = pl.DeviceIdType.MESH
CHUNKS = 8
PIECES = 6
f32 = jnp.float32
bf16 = jnp.bfloat16


def dot(a, b, left=1, right=0):
    return lax.dot_general(
        a, b, (((left,), (right,)), ((), ())), preferred_element_type=f32
    )


def kernel(
    groups, tm, rec_hbm, xw_hbm, bw_hbm, code_hbm, og_hbm, y_ref, x_out, bc_out,
    rec_ref, xw_ref, bw_ref, code_ref, og_ref, in_s, rec_all, rhs, own, give, given, give_d, given_d, hop_in, hop_out, entering, passed,
    gt, gall, pt, pbuf, qs, rbuf, fin, ylocal, glocal,
    rec_s, rec_r, e_s, e_r, h_s, h_r, p_s, p_r, g_s, g_r, c_s, c_r, z_s, z_r, o_s, o_r,
):
    heads, frames = code_ref.shape
    width = xw_ref.shape[1]
    head = width // heads
    state = bw_ref.shape[1] // 2
    piece, rows = fin.shape[2:]
    block = PIECES * piece
    chips = tm // 2
    unit = 1.0 / (32.0 * frames * tm)
    scale = (state * frames * tm) ** (-0.5)

    loads = []
    for n, (src, dst) in enumerate((
        (rec_hbm, rec_ref), (bw_hbm, bw_ref), (xw_hbm, xw_ref), (code_hbm, code_ref), (og_hbm, og_ref),
    )):
        load = pltpu.make_async_copy(src, dst, in_s.at[n])
        load.start()
        loads.append(load)

    d = lax.axis_index("dp")
    i = lax.axis_index("tm")
    z = i // 2
    core = i % 2
    partner = i + 1 - 2 * core

    barrier = pltpu.get_barrier_semaphore()

    def greet(dp_to, tm_to):
        pl.semaphore_signal(barrier, inc=1, device_id=(dp_to, tm_to), device_id_type=MESH)

    for k in range(1, groups):
        greet(lax.rem(d + k, groups), i)
    for k in range(1, chips):
        greet(d, lax.rem(z + k, chips) * 2 + core)
    greet(d, partner)

    loads[0].wait()
    rec = rec_ref[...]
    rec_all[d] = rec.astype(f32)
    pl.semaphore_wait(barrier, (groups - 1) + (chips - 1) + 1)

    def remote(src, dst, send, recv, dp_to, tm_to):
        return pltpu.make_async_remote_copy(
            src_ref=src, dst_ref=dst, send_sem=send, recv_sem=recv,
            device_id=(dp_to, tm_to), device_id_type=MESH,
        )

    rec_copies = []

    def send_rec(n, source, half, to, start=True):
        size = frames if half is None else frames // 2
        ref = rec_all.at[source, pl.ds((half or 0) * size, size)]
        copy = remote(ref, ref, rec_s.at[n], rec_r.at[n], to, i)
        if start:
            copy.start()
        rec_copies.append(copy)
        return copy

    square = groups == 4
    if square:
        beside = d + 1 - 2 * (d % 2)
        across = lax.rem(d + 2, groups)
        first_a = send_rec(0, d, 0, beside)
        first_b = send_rec(1, d, 1, across)
        second_b = send_rec(2, d, 1, beside, False)
        second_a = send_rec(3, d, 0, across, False)
        relay_a = send_rec(4, beside, 0, across, False)
        relay_b = send_rec(5, across, 1, beside, False)
    else:
        for k in range(1, groups):
            send_rec(k, d, None, lax.rem(d + k, groups))

    for load in loads[1:]:
        load.wait()
    mix = dot(rec, xw_ref[...]).astype(bf16)
    proj = dot(rec, bw_ref[...]).astype(bf16)
    inject, readout = proj[:, :state], proj[:, state:]
    og = og_ref[...]
    mix_t = mix.astype(f32).T
    cot_t = og.astype(f32).T
    proj_t = proj.astype(f32).T.astype(bf16)

    codes = code_ref[...].astype(f32)
    high = jnp.floor(codes * 0.125)
    low = codes - 8.0 * high
    spread = (
        lax.broadcasted_iota(jnp.int32, (heads, width), 1) // head
        == lax.broadcasted_iota(jnp.int32, (heads, width), 0)
    ).astype(f32)
    high_w, low_w = dot(high, spread, 0, 0), dot(low, spread, 0, 0)
    high_t, low_t = dot(spread, high, 0, 0), dot(spread, low, 0, 0)
    t_at = lax.broadcasted_iota(jnp.int32, (frames, frames), 0)
    s_at = lax.broadcasted_iota(jnp.int32, (frames, frames), 1)
    causal = t_at >= s_at
    tri = causal.astype(f32).astype(bf16)
    upper_tri = (t_at <= s_at).astype(f32).astype(bf16)
    sums = jnp.concatenate([upper_tri, jnp.ones((frames, frames), bf16)], axis=1)
    run = 8.0 * dot(tri, high_w.astype(bf16)) + dot(tri, low_w.astype(bf16))
    both = 8.0 * dot(high_t.astype(bf16), sums) + dot(low_t.astype(bf16), sums)
    run_t, total_t = both[:, :frames], both[:, frames:]
    decayed_t = jnp.exp(-unit * run_t)
    to_end_t = jnp.exp(-unit * (total_t - run_t))
    mix_end = (to_end_t * mix_t).astype(bf16)
    cot_dec = (decayed_t * cot_t).astype(bf16)
    ones = jnp.ones((frames, 128), f32)
    give_d[...] = jnp.exp(-unit * (8.0 * dot(high, ones) + dot(low, ones)))
    ends = dot(mix_end, inject)
    starts = dot(cot_dec, readout)

    forward = core == 1

    @pl.when(forward)
    def _():
        own[...] = ends
        give[...] = starts

    @pl.when(jnp.logical_not(forward))
    def _():
        own[...] = starts
        give[...] = ends

    part = width // CHUNKS
    per = heads // CHUNKS
    place = jnp.where(forward, z, chips - 1 - z)
    onward = lax.rem(jnp.where(forward, z + 1, z + chips - 1), chips) * 2 + core
    exchange = [remote(give_d, given_d, e_s.at[CHUNKS], e_r.at[CHUNKS], d, partner)]
    hops, passes = [], []
    for c in range(CHUNKS):
        at = pl.ds(c * part, part)
        exchange.append(remote(give.at[at], given.at[at], e_s.at[c], e_r.at[c], d, partner))
        hops.append(remote(hop_out.at[at], hop_in.at[at], h_s.at[c], h_r.at[c], d, onward))
        passes.append(remote(hop_in.at[at], passed.at[at], p_s.at[c], p_r.at[c], d, partner))
    for copy in exchange:
        copy.start()
    if square:
        second_b.start()
        second_a.start()

    def chain(chunks):
        if chunks[0] == 0:
            exchange[0].wait_recv()

        def factors(ref, c):
            return jnp.concatenate(
                [jnp.broadcast_to(ref[h:h + 1, :], (head, 128)) for h in range(c * per, (c + 1) * per)],
                axis=0,
            )

        for c in chunks:
            at = pl.ds(c * part, part)
            exchange[c + 1].wait_recv()

            @pl.when(place > 0)
            def _():
                hops[c].wait_recv()

            @pl.when(place == 0)
            def _():
                hop_in[at] = jnp.zeros((part, state), f32)

            inside = factors(given_d, c) * hop_in[at] + given[at]
            entering[at] = inside

            @pl.when(place < chips - 1)
            def _():
                hop_out[at] = factors(give_d, c) * inside + own[at]
                hops[c].start()

            passes[c].start()

    early = place < chips // 2
    late = jnp.logical_not(early)

    def relay():
        if square:
            first_a.wait_recv()
            relay_a.start()
            first_b.wait_recv()
            relay_b.start()

    @pl.when(early)
    def _():
        chain(range(CHUNKS))
        relay()

    scores = dot(readout, inject, 1, 1)
    cot_tb = cot_t.astype(bf16)
    pairs = jnp.zeros((frames, frames), f32)
    for h in range(heads):
        cols = slice(h * head, (h + 1) * head)
        gap = run[:, h * head:h * head + 1] - run_t[h * head:h * head + 1, :]
        decay = jnp.where(causal, jnp.exp(-unit * gap), 0.0)
        mixing = (decay * scores).astype(bf16)
        ylocal[:, cols] = dot(mixing, mix[:, cols])
        pairs = pairs + decay * dot(og[:, cols], mix[:, cols], 1, 1)
        glocal[cols, :] = dot(cot_tb[cols, :], mixing)
    pairs = pairs.astype(bf16)
    inj_local = dot(proj_t[state:], pairs)
    read_local = dot(proj_t[:state], pairs, 1, 1)

    pl.when(late)(relay)

    def rounded(a):
        return (scale * a).astype(bf16).astype(f32)

    g_copies = []

    def send_g(q):
        for k in range(1, groups):
            to = lax.rem(d + k, groups)
            at = pl.ds(pl.multiple_of((q * groups + to) * piece, 8), piece)
            copy = remote(gt.at[at], gall.at[d, q], g_s.at[q, k], g_r.at[q, k], to, i)
            copy.start()
            g_copies.append(copy)
        gall[d, q] = gt[pl.ds(pl.multiple_of((q * groups + d) * piece, 8), piece)]

    split = groups * piece
    adjs, carries = [], []
    early_pieces = width // split
    for q in range(early_pieces):
        at = slice(q * split, (q + 1) * split)
        chunks = range(q * split // part, (q + 1) * split // part)
        pl.when(late)(functools.partial(chain, chunks))
        for c in chunks:
            passes[c].wait_recv()
        mine, theirs = entering[at].astype(bf16), passed[at].astype(bf16)
        adjs.append(jnp.where(forward, theirs, mine))
        carries.append(jnp.where(forward, mine, theirs))
        gt[at] = rounded(to_end_t[at] * dot(adjs[q], inject, 1, 1) + glocal[at])
        send_g(q)
    adj_b = jnp.concatenate(adjs, axis=0)
    carry_b = jnp.concatenate(carries, axis=0)
    inj_grad = inj_local + dot(adj_b, mix_end, 0, 0)
    read_grad = read_local + dot(carry_b, cot_dec, 0, 0)
    gt[width:width + state] = rounded(inj_grad)
    gt[width + state:width + 2 * state] = rounded(read_grad)
    for q in range(early_pieces, PIECES):
        send_g(q)
    y_ref[...] = (
        jnp.exp(-unit * run) * dot(readout, carry_b, 1, 1) + ylocal[...]
    ).astype(bf16)
    for copy in rec_copies:
        if not (square and (copy is first_a or copy is first_b)):
            copy.wait_recv()
    for r in range(groups):
        rhs[r * frames:(r + 1) * frames] = rec_all[r].astype(bf16)

    c_copies, z_copies, o_copies = [], [], []

    def product(q):
        for copy in g_copies[q * (groups - 1):(q + 1) * (groups - 1)]:
            copy.wait_recv()
        lhs = jnp.concatenate([gall[r, q].astype(bf16) for r in range(groups)], axis=1)
        for zt in range(chips):
            prod = dot(lhs, rhs[:, zt * 2 * rows:(zt + 1) * 2 * rows])
            pt[0, q, zt] = prod[:, :rows]
            pt[1, q, zt] = prod[:, rows:]
        copy = remote(pt.at[1 - core, q], pbuf.at[q], c_s.at[q], c_r.at[q], d, partner)
        copy.start()
        c_copies.append(copy)

    def over_chips(q):
        c_copies[q].wait_recv()
        for k in range(1, chips):
            zt = lax.rem(z + k, chips)
            qs[q, k] = pt[core, q, zt] + pbuf[q, zt]
            copy = remote(qs.at[q, k], rbuf.at[q, k], z_s.at[q, k], z_r.at[q, k], d, zt * 2 + core)
            copy.start()
            z_copies.append(copy)

    def over_groups(q):
        total = pt[core, q, z] + pbuf[q, z]
        for k in range(1, chips):
            z_copies[q * (chips - 1) + k - 1].wait_recv()
            total = total + rbuf[q, k]
        fin[q, d] = total
        for k in range(1, groups):
            copy = remote(fin.at[q, d], fin.at[q, d], o_s.at[q, k], o_r.at[q, k],
                          lax.rem(d + k, groups), i)
            copy.start()
            o_copies.append(copy)

    for step in range(PIECES + 2):
        if step < PIECES:
            product(step)
        if 1 <= step <= PIECES:
            over_chips(step - 1)
        if step >= 2:
            over_groups(step - 2)
    for copy in o_copies:
        copy.wait_recv()
    whole = fin[...].reshape(groups * block, rows).T * ((groups * frames * tm) ** (-0.5))
    x_out[...] = whole[:, :width]
    bc_out[...] = whole[:, width:]

    for copy in rec_copies + exchange + passes + g_copies + c_copies + z_copies + o_copies:
        copy.wait_send()
    for copy in hops:
        pl.when(place < chips - 1)(copy.wait_send)


def body(records, x_weight, bc_weight, decay_codes, out_grad):
    signal = records[0]
    codes = decay_codes[0].T
    frames, model = signal.shape
    width = x_weight.shape[1]
    wide = width + bc_weight.shape[1]
    state = bc_weight.shape[1] // 2
    tm = lax.axis_size("tm")
    groups = lax.axis_size("dp")
    chips = tm // 2
    rows = model // tm
    piece = wide // groups // PIECES
    vmem = pl.BlockSpec(memory_space=pltpu.VMEM)

    def buf(*shape):
        return pltpu.VMEM(shape, f32)

    def sems(*n):
        return [pltpu.SemaphoreType.DMA(n), pltpu.SemaphoreType.DMA(n)]

    y, x_grad, bc_grad = pl.pallas_call(
        functools.partial(kernel, groups, tm),
        out_shape=(
            pltpu.VMEM((frames, width), bf16),
            pltpu.VMEM((rows, width), f32),
            pltpu.VMEM((rows, wide - width), f32),
        ),
        in_specs=[pl.BlockSpec(memory_space=pltpu.HBM)] * 5,
        out_specs=(vmem, vmem, vmem),
        scratch_shapes=[
            pltpu.VMEM((frames, model), bf16), pltpu.VMEM(x_weight.shape, bf16),
            pltpu.VMEM(bc_weight.shape, bf16), pltpu.VMEM(codes.shape, jnp.int32),
            pltpu.VMEM((frames, width), bf16), pltpu.SemaphoreType.DMA((5,)),
            buf(groups, frames, model), pltpu.VMEM((groups * frames, model), bf16),
            buf(width, state), buf(width, state), buf(width, state),
            buf(codes.shape[0], 128), buf(codes.shape[0], 128),
            buf(width, state), buf(width, state), buf(width, state), buf(width, state),
            buf(wide, frames), buf(groups, PIECES, piece, frames),
            buf(2, PIECES, chips, piece, rows), buf(PIECES, chips, piece, rows),
            buf(PIECES, chips, piece, rows), buf(PIECES, chips, piece, rows),
            buf(PIECES, groups, piece, rows), buf(frames, width), buf(width, frames),
            *sems(max(groups, 6)), *sems(CHUNKS + 1), *sems(CHUNKS), *sems(CHUNKS), *sems(PIECES, groups),
            *sems(PIECES), *sems(PIECES, chips), *sems(PIECES, groups),
        ],
        compiler_params=pltpu.CompilerParams(
            collective_id=0, has_side_effects=True, vmem_limit_bytes=60 * 1024 * 1024
        ),
    )(signal, x_weight, bc_weight, codes, out_grad[0])
    return (y[None], x_grad, bc_grad)


def solution(mesh):
    return jax.shard_map(
        body,
        mesh=mesh,
        in_specs=(P("dp", "tm", None), P(), P(), P("dp", "tm", None), P("dp", "tm", None)),
        out_specs=(P("dp", "tm", None), P("tm", None), P("tm", None)),
        check_vma=False,
    )
```

```python
import functools

import jax
import jax.numpy as jnp
from jax import lax
from jax.experimental import pallas as pl
from jax.experimental.pallas import tpu as pltpu
from jax.sharding import PartitionSpec as P

MESH = pl.DeviceIdType.MESH
CHUNKS = 8
PIECES = 3
f32 = jnp.float32
bf16 = jnp.bfloat16


def dot(a, b, left=1, right=0):
    return lax.dot_general(
        a, b, (((left,), (right,)), ((), ())), preferred_element_type=f32
    )


def kernel(
    groups, tm, rec_hbm, xw_hbm, bw_hbm, code_hbm, og_hbm, y_ref, x_out, bc_out,
    rec_ref, xw_ref, bw_ref, code_ref, og_ref, in_s, rec_all, rhs, own, give, given, give_d, given_d, hop_in, hop_out, entering, passed,
    gt, gall, pt, pbuf, qs, rbuf, fin, ylocal, glocal,
    rec_s, rec_r, e_s, e_r, h_s, h_r, p_s, p_r, g_s, g_r, c_s, c_r, z_s, z_r, o_s, o_r,
):
    heads, frames = code_ref.shape
    width = xw_ref.shape[1]
    head = width // heads
    state = bw_ref.shape[1] // 2
    piece, rows = fin.shape[2:]
    block = PIECES * piece
    chips = tm // 2
    unit = 1.0 / (32.0 * frames * tm)
    scale = (state * frames * tm) ** (-0.5)

    loads = []
    for n, (src, dst) in enumerate((
        (rec_hbm, rec_ref), (bw_hbm, bw_ref), (xw_hbm, xw_ref), (code_hbm, code_ref), (og_hbm, og_ref),
    )):
        load = pltpu.make_async_copy(src, dst, in_s.at[n])
        load.start()
        loads.append(load)

    d = lax.axis_index("dp")
    i = lax.axis_index("tm")
    z = i // 2
    core = i % 2
    partner = i + 1 - 2 * core

    barrier = pltpu.get_barrier_semaphore()

    def greet(dp_to, tm_to):
        pl.semaphore_signal(barrier, inc=1, device_id=(dp_to, tm_to), device_id_type=MESH)

    for k in range(1, groups):
        greet(lax.rem(d + k, groups), i)
    for k in range(1, chips):
        greet(d, lax.rem(z + k, chips) * 2 + core)
    greet(d, partner)

    loads[0].wait()
    rec = rec_ref[...]
    rec_all[d] = rec.astype(f32)
    pl.semaphore_wait(barrier, (groups - 1) + (chips - 1) + 1)

    def remote(src, dst, send, recv, dp_to, tm_to):
        return pltpu.make_async_remote_copy(
            src_ref=src, dst_ref=dst, send_sem=send, recv_sem=recv,
            device_id=(dp_to, tm_to), device_id_type=MESH,
        )

    rec_copies = []

    def send_rec(n, source, half, to, start=True):
        size = frames if half is None else frames // 2
        ref = rec_all.at[source, pl.ds((half or 0) * size, size)]
        copy = remote(ref, ref, rec_s.at[n], rec_r.at[n], to, i)
        if start:
            copy.start()
        rec_copies.append(copy)
        return copy

    square = groups == 4
    if square:
        beside = d + 1 - 2 * (d % 2)
        across = lax.rem(d + 2, groups)
        first_a = send_rec(0, d, 0, beside)
        first_b = send_rec(1, d, 1, across)
        second_b = send_rec(2, d, 1, beside, False)
        second_a = send_rec(3, d, 0, across, False)
        relay_a = send_rec(4, beside, 0, across, False)
        relay_b = send_rec(5, across, 1, beside, False)
    else:
        for k in range(1, groups):
            send_rec(k, d, None, lax.rem(d + k, groups))

    for load in loads[1:]:
        load.wait()
    mix = dot(rec, xw_ref[...]).astype(bf16)
    proj = dot(rec, bw_ref[...]).astype(bf16)
    inject, readout = proj[:, :state], proj[:, state:]
    og = og_ref[...]
    mix_t = mix.astype(f32).T
    cot_t = og.astype(f32).T
    proj_t = proj.astype(f32).T.astype(bf16)

    codes = code_ref[...].astype(f32)
    high = jnp.floor(codes * 0.125)
    low = codes - 8.0 * high
    spread = (
        lax.broadcasted_iota(jnp.int32, (heads, width), 1) // head
        == lax.broadcasted_iota(jnp.int32, (heads, width), 0)
    ).astype(f32)
    high_w, low_w = dot(high, spread, 0, 0), dot(low, spread, 0, 0)
    high_t, low_t = dot(spread, high, 0, 0), dot(spread, low, 0, 0)
    t_at = lax.broadcasted_iota(jnp.int32, (frames, frames), 0)
    s_at = lax.broadcasted_iota(jnp.int32, (frames, frames), 1)
    causal = t_at >= s_at
    tri = causal.astype(f32).astype(bf16)
    upper_tri = (t_at <= s_at).astype(f32).astype(bf16)
    sums = jnp.concatenate([upper_tri, jnp.ones((frames, frames), bf16)], axis=1)
    run = 8.0 * dot(tri, high_w.astype(bf16)) + dot(tri, low_w.astype(bf16))
    both = 8.0 * dot(high_t.astype(bf16), sums) + dot(low_t.astype(bf16), sums)
    run_t, total_t = both[:, :frames], both[:, frames:]
    decayed_t = jnp.exp(-unit * run_t)
    to_end_t = jnp.exp(-unit * (total_t - run_t))
    mix_end = (to_end_t * mix_t).astype(bf16)
    cot_dec = (decayed_t * cot_t).astype(bf16)
    ones = jnp.ones((frames, 128), f32)
    give_d[...] = jnp.exp(-unit * (8.0 * dot(high, ones) + dot(low, ones)))
    ends = dot(mix_end, inject)
    starts = dot(cot_dec, readout)

    forward = core == 1

    @pl.when(forward)
    def _():
        own[...] = ends
        give[...] = starts

    @pl.when(jnp.logical_not(forward))
    def _():
        own[...] = starts
        give[...] = ends

    part = width // CHUNKS
    per = heads // CHUNKS
    place = jnp.where(forward, z, chips - 1 - z)
    onward = lax.rem(jnp.where(forward, z + 1, z + chips - 1), chips) * 2 + core
    exchange = [remote(give_d, given_d, e_s.at[CHUNKS], e_r.at[CHUNKS], d, partner)]
    hops, passes = [], []
    for c in range(CHUNKS):
        at = pl.ds(c * part, part)
        exchange.append(remote(give.at[at], given.at[at], e_s.at[c], e_r.at[c], d, partner))
        hops.append(remote(hop_out.at[at], hop_in.at[at], h_s.at[c], h_r.at[c], d, onward))
        passes.append(remote(hop_in.at[at], passed.at[at], p_s.at[c], p_r.at[c], d, partner))
    for copy in exchange:
        copy.start()
    if square:
        second_b.start()
        second_a.start()

    def chain(chunks):
        if chunks[0] == 0:
            exchange[0].wait_recv()

        def factors(ref, c):
            return jnp.concatenate(
                [jnp.broadcast_to(ref[h:h + 1, :], (head, 128)) for h in range(c * per, (c + 1) * per)],
                axis=0,
            )

        for c in chunks:
            at = pl.ds(c * part, part)
            exchange[c + 1].wait_recv()

            @pl.when(place > 0)
            def _():
                hops[c].wait_recv()

            @pl.when(place == 0)
            def _():
                hop_in[at] = jnp.zeros((part, state), f32)

            inside = factors(given_d, c) * hop_in[at] + given[at]
            entering[at] = inside

            @pl.when(place < chips - 1)
            def _():
                hop_out[at] = factors(give_d, c) * inside + own[at]
                hops[c].start()

            passes[c].start()

    early = place < chips // 2
    late = jnp.logical_not(early)

    def relay():
        if square:
            first_a.wait_recv()
            relay_a.start()
            first_b.wait_recv()
            relay_b.start()

    @pl.when(early)
    def _():
        chain(range(CHUNKS))
        relay()

    scores = dot(readout, inject, 1, 1)
    cot_tb = cot_t.astype(bf16)
    pairs = jnp.zeros((frames, frames), f32)
    for h in range(heads):
        cols = slice(h * head, (h + 1) * head)
        gap = run[:, h * head:h * head + 1] - run_t[h * head:h * head + 1, :]
        decay = jnp.where(causal, jnp.exp(-unit * gap), 0.0)
        mixing = (decay * scores).astype(bf16)
        ylocal[:, cols] = dot(mixing, mix[:, cols])
        pairs = pairs + decay * dot(og[:, cols], mix[:, cols], 1, 1)
        glocal[cols, :] = dot(cot_tb[cols, :], mixing)
    pairs = pairs.astype(bf16)
    inj_local = dot(proj_t[state:], pairs)
    read_local = dot(proj_t[:state], pairs, 1, 1)

    pl.when(late)(relay)

    def rounded(a):
        return (scale * a).astype(bf16).astype(f32)

    g_copies = []

    def send_g(q):
        for k in range(1, groups):
            to = lax.rem(d + k, groups)
            at = pl.ds(pl.multiple_of((q * groups + to) * piece, 8), piece)
            copy = remote(gt.at[at], gall.at[d, q], g_s.at[q, k], g_r.at[q, k], to, i)
            copy.start()
            g_copies.append(copy)
        gall[d, q] = gt[pl.ds(pl.multiple_of((q * groups + d) * piece, 8), piece)]

    split = groups * piece
    adjs, carries = [], []
    for q in range(PIECES - 1):
        at = slice(q * split, (q + 1) * split)
        chunks = range(q * split // part, (q + 1) * split // part)
        pl.when(late)(functools.partial(chain, chunks))
        for c in chunks:
            passes[c].wait_recv()
        mine, theirs = entering[at].astype(bf16), passed[at].astype(bf16)
        adjs.append(jnp.where(forward, theirs, mine))
        carries.append(jnp.where(forward, mine, theirs))
        gt[at] = rounded(to_end_t[at] * dot(adjs[q], inject, 1, 1) + glocal[at])
        send_g(q)
    adj_b = jnp.concatenate(adjs, axis=0)
    carry_b = jnp.concatenate(carries, axis=0)
    inj_grad = inj_local + dot(adj_b, mix_end, 0, 0)
    read_grad = read_local + dot(carry_b, cot_dec, 0, 0)
    gt[width:width + state] = rounded(inj_grad)
    gt[width + state:width + 2 * state] = rounded(read_grad)
    send_g(PIECES - 1)
    y_ref[...] = (
        jnp.exp(-unit * run) * dot(readout, carry_b, 1, 1) + ylocal[...]
    ).astype(bf16)
    for copy in rec_copies:
        if not (square and (copy is first_a or copy is first_b)):
            copy.wait_recv()
    for r in range(groups):
        rhs[r * frames:(r + 1) * frames] = rec_all[r].astype(bf16)

    c_copies, z_copies, o_copies = [], [], []

    def product(q):
        for copy in g_copies[q * (groups - 1):(q + 1) * (groups - 1)]:
            copy.wait_recv()
        lhs = jnp.concatenate([gall[r, q].astype(bf16) for r in range(groups)], axis=1)
        for zt in range(chips):
            prod = dot(lhs, rhs[:, zt * 2 * rows:(zt + 1) * 2 * rows])
            pt[0, q, zt] = prod[:, :rows]
            pt[1, q, zt] = prod[:, rows:]
        copy = remote(pt.at[1 - core, q], pbuf.at[q], c_s.at[q], c_r.at[q], d, partner)
        copy.start()
        c_copies.append(copy)

    def over_chips(q):
        c_copies[q].wait_recv()
        for k in range(1, chips):
            zt = lax.rem(z + k, chips)
            qs[q, k] = pt[core, q, zt] + pbuf[q, zt]
            copy = remote(qs.at[q, k], rbuf.at[q, k], z_s.at[q, k], z_r.at[q, k], d, zt * 2 + core)
            copy.start()
            z_copies.append(copy)

    def over_groups(q):
        total = pt[core, q, z] + pbuf[q, z]
        for k in range(1, chips):
            z_copies[q * (chips - 1) + k - 1].wait_recv()
            total = total + rbuf[q, k]
        fin[q, d] = total
        for k in range(1, groups):
            copy = remote(fin.at[q, d], fin.at[q, d], o_s.at[q, k], o_r.at[q, k],
                          lax.rem(d + k, groups), i)
            copy.start()
            o_copies.append(copy)

    for step in range(PIECES + 2):
        if 1 <= step <= PIECES:
            over_chips(step - 1)
        if step < PIECES:
            product(step)
        if step >= 2:
            over_groups(step - 2)
    for copy in o_copies:
        copy.wait_recv()
    whole = fin[...].reshape(groups * block, rows).T * ((groups * frames * tm) ** (-0.5))
    x_out[...] = whole[:, :width]
    bc_out[...] = whole[:, width:]

    for copy in rec_copies + exchange + passes + g_copies + c_copies + z_copies + o_copies:
        copy.wait_send()
    for copy in hops:
        pl.when(place < chips - 1)(copy.wait_send)


def body(records, x_weight, bc_weight, decay_codes, out_grad):
    signal = records[0]
    codes = decay_codes[0].T
    frames, model = signal.shape
    width = x_weight.shape[1]
    wide = width + bc_weight.shape[1]
    state = bc_weight.shape[1] // 2
    tm = lax.axis_size("tm")
    groups = lax.axis_size("dp")
    chips = tm // 2
    rows = model // tm
    piece = wide // groups // PIECES
    vmem = pl.BlockSpec(memory_space=pltpu.VMEM)

    def buf(*shape):
        return pltpu.VMEM(shape, f32)

    def sems(*n):
        return [pltpu.SemaphoreType.DMA(n), pltpu.SemaphoreType.DMA(n)]

    y, x_grad, bc_grad = pl.pallas_call(
        functools.partial(kernel, groups, tm),
        out_shape=(
            pltpu.VMEM((frames, width), bf16),
            pltpu.VMEM((rows, width), f32),
            pltpu.VMEM((rows, wide - width), f32),
        ),
        in_specs=[pl.BlockSpec(memory_space=pltpu.HBM)] * 5,
        out_specs=(vmem, vmem, vmem),
        scratch_shapes=[
            pltpu.VMEM((frames, model), bf16), pltpu.VMEM(x_weight.shape, bf16),
            pltpu.VMEM(bc_weight.shape, bf16), pltpu.VMEM(codes.shape, jnp.int32),
            pltpu.VMEM((frames, width), bf16), pltpu.SemaphoreType.DMA((5,)),
            buf(groups, frames, model), pltpu.VMEM((groups * frames, model), bf16),
            buf(width, state), buf(width, state), buf(width, state),
            buf(codes.shape[0], 128), buf(codes.shape[0], 128),
            buf(width, state), buf(width, state), buf(width, state), buf(width, state),
            buf(wide, frames), buf(groups, PIECES, piece, frames),
            buf(2, PIECES, chips, piece, rows), buf(PIECES, chips, piece, rows),
            buf(PIECES, chips, piece, rows), buf(PIECES, chips, piece, rows),
            buf(PIECES, groups, piece, rows), buf(frames, width), buf(width, frames),
            *sems(max(groups, 6)), *sems(CHUNKS + 1), *sems(CHUNKS), *sems(CHUNKS), *sems(PIECES, groups),
            *sems(PIECES), *sems(PIECES, chips), *sems(PIECES, groups),
        ],
        compiler_params=pltpu.CompilerParams(
            collective_id=0, has_side_effects=True, vmem_limit_bytes=60 * 1024 * 1024
        ),
    )(signal, x_weight, bc_weight, codes, out_grad[0])
    return (y[None], x_grad, bc_grad)


def solution(mesh):
    return jax.shard_map(
        body,
        mesh=mesh,
        in_specs=(P("dp", "tm", None), P(), P(), P("dp", "tm", None), P("dp", "tm", None)),
        out_specs=(P("dp", "tm", None), P("tm", None), P("tm", None)),
        check_vma=False,
    )
```
